256 devices in a mesh: space: 64 (over x, z, core), tm: 4 (over y).
Axes of the slice: x: 4, y: 4, z: 8, core: 2. Of those that a mesh axis runs over, the one named last changes fastest.
Arguments:
- queries: bfloat16 [4, 16384, 1024], P('tm', 'space'), may hold values from -6 to 6
- key_vectors: bfloat16 [4, 16384, 1024], P('tm', 'space'), may hold values from -6 to 6
- value_vectors: bfloat16 [4, 16384, 1024], P('tm', 'space'), may hold values from -6 to 6
- query_time: bfloat16 [4, 16384, 1024], P('tm', 'space'), may hold values from -6 to 6
- key_time: bfloat16 [4, 16384, 1024], P('tm', 'space'), may hold values from -6 to 6
- out_grad: bfloat16 [4, 16384, 1024], P('tm', 'space'), may hold values from -6 to 6
- fluid_mask: int32 [128], replicated, may hold values from 0 to 1, as said below
- occupancy: int32 [16384], replicated, may hold values 0 or 1
- key_lists: int32 [64, 2, 4, 2], replicated, may hold values from 0 to 63, as said below
Outputs:
- query_grad: bfloat16 [4, 16384, 1024], P('tm', 'space')
- key_grad: bfloat16 [4, 16384, 1024], P('tm', 'space')
- value_grad: bfloat16 [4, 16384, 1024], P('tm', 'space')
- query_time_grad: bfloat16 [4, 16384, 1024], P('tm', 'space')
- key_time_grad: bfloat16 [4, 16384, 1024], P('tm', 'space')
The draws below stay inside these ranges and needn't reach their ends.
Inputs may be any that keep to these rules, and one draw needn't show every extreme that they name: Every domain holds at least one block with fluid_mask 1. key_lists[s, b] holds first the 2 blocks of domain s in the order b, b + 1, ... modulo 2, then 1 distinct blocks of domain (s - 1) mod 64, then 1 distinct blocks of domain (s + 1) mod 64.
All inputs are finite; a program needn't handle non-finite values.
Results may differ from the reference program's by a relative error of at most 0.02.
Values may be sent and summed in bfloat16 or wider, within the bound.
No kernel may reach another device: no remote copies, remote signals or barrier semaphores. Data moves between devices by JAX's collectives and lax.ppermute only.
A program may use at most 128 MiB of HBM per device.

```python
import jax
import jax.numpy as jnp
from jax import lax

BLOCK = 128
BLOCKS_DEV = 2
H = 16
HD = 64
D = 1024
NSIDE = 1
NB = 4
TOK_DEV = 256
DOMAINS = 64
TSTEPS = 4
PATCHES = 16384


def drawn_pair(key, salt):
    first_key, second_key = jax.random.split(jax.random.fold_in(key, salt), 2)
    shape = (TSTEPS, PATCHES, D)
    first = jax.random.normal(first_key, shape, jnp.float32)
    second = jax.random.normal(second_key, shape, jnp.float32)
    return (jnp.clip(first, -6.0, 6.0), jnp.clip(second, -6.0, 6.0))


def draw_queries(key, part):
    return drawn_pair(key, 11)[0].astype(jnp.bfloat16)


def draw_key_vectors(key, part):
    return drawn_pair(key, 11)[1].astype(jnp.bfloat16)


def draw_query_time(key, part):
    return drawn_pair(key, 13)[0].astype(jnp.bfloat16)


def draw_key_time(key, part):
    return drawn_pair(key, 13)[1].astype(jnp.bfloat16)


def draw_fluid_mask(key, part):
    mask_key, pick_key = jax.random.split(jax.random.fold_in(key, 23))
    flags = (jax.random.randint(mask_key, (DOMAINS, BLOCKS_DEV), 0, 4) < 3).astype(jnp.int32)
    chosen = jax.random.randint(pick_key, (DOMAINS, 1), 0, BLOCKS_DEV)
    forced = (jnp.arange(BLOCKS_DEV, dtype=jnp.int32)[None, :] == chosen).astype(jnp.int32)
    return jnp.maximum(flags, forced).reshape(-1).astype(jnp.int32)


def draw_key_lists(key, part):
    left_key, right_key = jax.random.split(jax.random.fold_in(key, 17))
    domain = jnp.arange(DOMAINS, dtype=jnp.int32)[:, None, None]
    block = jnp.arange(BLOCKS_DEV, dtype=jnp.int32)[None, :, None]
    stride = jnp.arange(BLOCKS_DEV, dtype=jnp.int32)[None, None, :]
    own_blocks = jnp.broadcast_to((block + stride) % BLOCKS_DEV, (DOMAINS, BLOCKS_DEV, BLOCKS_DEV))

    def pick(sub_key):
        scores = jax.random.randint(sub_key, (DOMAINS, BLOCKS_DEV, BLOCKS_DEV), 0, 1 << 16) * BLOCKS_DEV + stride
        return lax.top_k(scores, NSIDE)[1].astype(jnp.int32)
    block_field = jnp.concatenate([own_blocks, pick(left_key), pick(right_key)], axis=2)
    owner_field = jnp.concatenate([jnp.broadcast_to(domain, (DOMAINS, BLOCKS_DEV, BLOCKS_DEV)), jnp.broadcast_to((domain - 1 + DOMAINS) % DOMAINS, (DOMAINS, BLOCKS_DEV, NSIDE)), jnp.broadcast_to((domain + 1) % DOMAINS, (DOMAINS, BLOCKS_DEV, NSIDE))], axis=2)
    return jnp.stack([owner_field, block_field], axis=-1).astype(jnp.int32)


def with_ends(result, rng, least, largest):
    place = [jax.random.randint(jax.random.fold_in(rng, axis), (), 0, length) for axis, length in enumerate(result.shape)]
    longest = result.shape.index(max(result.shape))
    next_to = place[:longest] + [(place[longest] + 1) % result.shape[longest]] + place[longest + 1:]
    return result.at[tuple(place)].set(least).at[tuple(next_to)].set(largest)


def block_scale(rng, extent, pieces, low, largest):
    def one(dim, shards_of):
        heights = jax.random.uniform(jax.random.fold_in(jax.random.fold_in(rng, 6), dim), (shards_of,), jnp.float32, low / len(pieces), largest / len(pieces))
        return jnp.repeat(jnp.exp(heights), extent[dim] // shards_of).reshape((-1,) + (1,) * (len(extent) - dim - 1))

    level = one(*pieces[0])
    for cut in pieces[1:]:
        level = level * one(*cut)
    return level


def bell_draw(stream_key, shape, scale, bound, shards=(), kind=jnp.bfloat16):
    entries = scale * jax.random.normal(stream_key, shape, jnp.float32)
    if shards:
        entries = entries * block_scale(stream_key, shape, shards, -0.22, 0.18)
    return jnp.clip(entries, -bound, bound).astype(kind)


def setup_inputs(seed: int = 0) -> dict:
    key_of = jax.random.split(jax.random.key(seed), 10)
    return {
        "queries": draw_queries(jax.random.fold_in(key_of[9], 71), 0),
        "key_vectors": draw_key_vectors(jax.random.fold_in(key_of[9], 71), 0),
        "value_vectors": bell_draw(key_of[2], (TSTEPS, PATCHES, D), 1.0, 6.0, ((0, 4), (1, 64))),
        "query_time": draw_query_time(jax.random.fold_in(key_of[9], 71), 0),
        "key_time": draw_key_time(jax.random.fold_in(key_of[9], 71), 0),
        "out_grad": bell_draw(key_of[5], (TSTEPS, PATCHES, D), 1.0, 6.0, ((0, 4), (1, 64))),
        "fluid_mask": draw_fluid_mask(jax.random.fold_in(key_of[9], 71), 0),
        "occupancy": with_ends((jax.random.randint(key_of[7], (PATCHES,), 0, 4) < 1).astype(jnp.int32), jax.random.fold_in(key_of[7], 1), 0, 1),
        "key_lists": draw_key_lists(jax.random.fold_in(key_of[9], 71), 0),
    }


def rounded(matrix):
    return lax.optimization_barrier(matrix.astype(jnp.bfloat16)).astype(jnp.float32)


def split_heads(matrix, heads):
    return matrix.reshape(matrix.shape[0], heads, matrix.shape[1] // heads).astype(jnp.float32)


def attend_forward(query_rows, key_rows, value_rows, live, heads, scale):
    query_heads = split_heads(query_rows, heads)
    key_heads = split_heads(key_rows, heads)
    value_heads = split_heads(value_rows, heads)
    scores = jnp.einsum("qhd,khd->hqk", query_heads, key_heads) * scale
    usable = live[None, None, :] > 0
    highest = jnp.maximum(jnp.max(jnp.where(usable, scores, -1e30), axis=-1), 0.0)
    weights = jnp.where(usable, jnp.exp(scores - highest[..., None]), 0.0)
    total = jnp.exp(-highest) + jnp.sum(weights, axis=-1)
    probs = rounded(weights / total[..., None])
    output = jnp.einsum("hqk,khd->qhd", probs, value_heads)
    return output.reshape(query_rows.shape).astype(jnp.bfloat16), highest + jnp.log(total)


def attend_backward(query_rows, grad_rows, logsum, delta, key_rows, value_rows, live, heads, scale):
    query_heads = split_heads(query_rows, heads)
    grad_heads = split_heads(grad_rows, heads)
    key_heads = split_heads(key_rows, heads)
    value_heads = split_heads(value_rows, heads)
    scores = jnp.einsum("qhd,khd->hqk", query_heads, key_heads) * scale
    usable = live[None, None, :] > 0
    probs = jnp.where(usable, jnp.exp(scores - logsum[..., None]), 0.0)
    dprobs = jnp.einsum("qhd,khd->hqk", grad_heads, value_heads)
    dscores = rounded(probs * (dprobs - delta[..., None]))
    query_part = jnp.einsum("hqk,khd->qhd", dscores, key_heads) * scale
    key_part = jnp.einsum("hqk,qhd->khd", dscores, query_heads) * scale
    value_part = jnp.einsum("hqk,qhd->khd", rounded(probs), grad_heads)
    return (query_part.reshape(query_rows.shape), key_part.reshape(key_rows.shape),
            value_part.reshape(key_rows.shape))


def temporal_grads(states, time_queries, time_keys, grads, heads, scale):
    steps, count, width = states.shape
    shape = (steps, count, heads, width // heads)
    query_heads = time_queries.astype(jnp.float32).reshape(shape)
    key_heads = time_keys.astype(jnp.float32).reshape(shape)
    state_heads = states.astype(jnp.float32).reshape(shape)
    grad_heads = grads.astype(jnp.float32).reshape(shape)
    scores = jnp.einsum("trhd,urhd->rhtu", query_heads, key_heads) * scale
    attn = jax.nn.softmax(scores, axis=-1)
    carried = jnp.einsum("rhtu,trhd->urhd", attn, grad_heads)
    state_grad = (grad_heads + carried).reshape(states.shape).astype(jnp.bfloat16)
    dattn = jnp.einsum("trhd,urhd->rhtu", grad_heads, state_heads)
    dscores = attn * (dattn - jnp.sum(attn * dattn, axis=-1, keepdims=True))
    query_grad = (jnp.einsum("rhtu,urhd->trhd", dscores, key_heads) * scale).reshape(states.shape)
    key_grad = (jnp.einsum("rhtu,trhd->urhd", dscores, query_heads) * scale).reshape(states.shape)
    return state_grad, query_grad.astype(jnp.bfloat16), key_grad.astype(jnp.bfloat16)


def reference(queries, key_vectors, value_vectors, query_time, key_time, out_grad, fluid_mask, occupancy, key_lists):
    scale = HD ** -0.5
    live_all = (1 - occupancy).astype(jnp.float32)
    offsets = jnp.arange(BLOCK, dtype=jnp.int32)
    flat_lists = key_lists.reshape(DOMAINS * BLOCKS_DEV, NB, 2)
    pairs = jnp.arange(DOMAINS * BLOCKS_DEV, dtype=jnp.int32)

    def key_index(listed):
        starts = listed[:, 0] * TOK_DEV + listed[:, 1] * BLOCK
        return (starts[:, None] + offsets[None, :]).reshape(-1).astype(jnp.int32)

    def forward_time(operands):
        query_step, key_step, value_step = operands

        def one_block(pair):
            index = key_index(flat_lists[pair])
            query_rows = lax.dynamic_slice_in_dim(query_step, (pair * BLOCK).astype(jnp.int32), BLOCK, 0)
            output, logsum = attend_forward(query_rows, key_step[index], value_step[index], live_all[index], H, scale)
            output = jnp.where(fluid_mask[pair] > 0, output, jnp.zeros_like(output))
            return output, logsum

        outputs, logsums = lax.map(one_block, pairs)
        return outputs.reshape(PATCHES, D), logsums

    states, logsums = lax.map(forward_time, (queries, key_vectors, value_vectors))

    def temporal_domain(domain):
        start = (domain * TOK_DEV).astype(jnp.int32)

        def take(matrix):
            return lax.dynamic_slice_in_dim(matrix, start, TOK_DEV, 1)

        return temporal_grads(take(states), take(query_time), take(key_time), take(out_grad), H, scale)

    domain_ids = jnp.arange(DOMAINS, dtype=jnp.int32)
    state_grads, query_time_grad, key_time_grad = lax.map(temporal_domain, domain_ids)

    def regroup(matrix):
        return matrix.transpose(1, 0, 2, 3).reshape(TSTEPS, PATCHES, D)

    state_grads = regroup(state_grads)

    def backward_time(operands):
        query_step, key_step, value_step, state_step, grad_step, logsum_step = operands

        def one_block(totals, pair):
            index = key_index(flat_lists[pair])
            start = (pair * BLOCK).astype(jnp.int32)
            query_rows = lax.dynamic_slice_in_dim(query_step, start, BLOCK, 0)
            grad_rows = lax.dynamic_slice_in_dim(grad_step, start, BLOCK, 0)
            state_rows = lax.dynamic_slice_in_dim(state_step, start, BLOCK, 0)
            product = grad_rows.astype(jnp.float32) * state_rows.astype(jnp.float32)
            delta = jnp.sum(product.reshape(BLOCK, H, HD), axis=-1).T
            query_part, key_part, value_part = attend_backward(
                query_rows, grad_rows, logsum_step[pair], delta, key_step[index], value_step[index],
                live_all[index], H, scale)
            keep = fluid_mask[pair] > 0
            query_part = jnp.where(keep, query_part, 0.0)
            key_part = jnp.where(keep, key_part, 0.0)
            value_part = jnp.where(keep, value_part, 0.0)
            return (totals[0].at[index].add(key_part), totals[1].at[index].add(value_part)), query_part

        empty = jnp.zeros((PATCHES, D), jnp.float32)
        totals, query_parts = lax.scan(one_block, (empty, empty), pairs)
        return (query_parts.reshape(PATCHES, D).astype(jnp.bfloat16), totals[0].astype(jnp.bfloat16),
                totals[1].astype(jnp.bfloat16))

    query_grad, key_grad, value_grad = lax.map(
        backward_time, (queries, key_vectors, value_vectors, states, state_grads, logsums))
    return query_grad, key_grad, value_grad, regroup(query_time_grad), regroup(key_time_grad)
```

```python
import functools

import jax
import jax.numpy as jnp
from jax import lax
from jax.experimental import pallas as pl
from jax.experimental.pallas import tpu as pltpu
from jax.sharding import PartitionSpec as P

BLOCK = 128
H = 16
HD = 64
D = 1024
TOK = 256
QUARTER = 64
PAIRS = 8
SCALE = HD**-0.5
NEG = -1e30
F32 = jnp.float32
BF16 = jnp.bfloat16

VMEM_SPEC = pl.BlockSpec(memory_space=pltpu.VMEM)
SMEM_SPEC = pl.BlockSpec(memory_space=pltpu.SMEM)


def dot(a, b):
    return jnp.dot(a, b, preferred_element_type=F32)


def kernel_params(mib):
    return pltpu.CompilerParams(vmem_limit_bytes=mib * 1024 * 1024)


def cost(flops, nbytes):
    return pl.CostEstimate(flops=flops, bytes_accessed=nbytes, transcendentals=0)


def transposed(block):
    return block.astype(F32).T.astype(BF16)


def head_rows(block):
    row = lax.broadcasted_iota(jnp.int32, block.shape, 0)
    zero = jnp.zeros_like(block)
    return jnp.where(row < HD, block, zero), jnp.where(row < HD, zero, block)


def head_lanes(block):
    lane = lax.broadcasted_iota(jnp.int32, block.shape, 1)
    zero = jnp.zeros_like(block)
    return jnp.where(lane < HD, block, zero), jnp.where(lane < HD, zero, block)


def grouped_lanes(block_t):
    first, second = head_rows(block_t)
    return jnp.concatenate(
        [first[:, :BLOCK], second[:, :BLOCK], first[:, BLOCK:], second[:, BLOCK:]], axis=1
    )


def grouped_rows(block):
    first, second = head_lanes(block)
    return jnp.concatenate([first[:BLOCK], second[:BLOCK], first[BLOCK:], second[BLOCK:]], axis=0)


def stage_kernel(place, *refs):
    ins, outs = refs[:9], refs[9:]
    for d in range(3):
        for a in range(3):
            outs[d][a] = ins[d * 3 + a][...]


def stage(place, arrays):
    specs, operands = [], []
    for d in (1, 2, 3):
        for array in arrays:
            specs.append(
                pl.BlockSpec((QUARTER, D), functools.partial(lambda d, i, s: ((s[0] + d) % 4, 0), d))
            )
            operands.append(array)
    return pl.pallas_call(
        stage_kernel,
        grid_spec=pltpu.PrefetchScalarGridSpec(
            num_scalar_prefetch=1,
            grid=(1,),
            in_specs=specs,
            out_specs=[pl.BlockSpec((3, QUARTER, D), lambda i, s: (0, 0, 0))] * 3,
        ),
        out_shape=[jax.ShapeDtypeStruct((3, QUARTER, D), BF16)] * 3,
        compiler_params=kernel_params(24),
        cost_estimate=cost(0, 3 << 20),
        name="stage_time",
    )(place, *operands)


def listed(place, lists, side):
    return [lists[b * 4 + 2 + side] for b in range(2)]


def neighbour_rows(low_ref, high_ref, low_ids, high_ids, b, lanes):
    low = low_ref[pl.ds(pl.multiple_of(low_ids[b] * BLOCK, BLOCK), BLOCK), lanes]
    high = high_ref[pl.ds(pl.multiple_of(high_ids[b] * BLOCK, BLOCK), BLOCK), lanes]
    return jnp.concatenate([low, high], axis=0)


def forward_kernel(
    place, lists, fluid, occ, q, k, v, k_low, v_low, k_high, v_high,
    states, p1, p2, p3, probs, states_t, bias, scratch,
):
    me, dom = place[0], place[1]
    low_dom, high_dom = lax.rem(dom + 63, 64), lax.rem(dom + 1, 64)
    low_ids, high_ids = listed(place, lists, 0), listed(place, lists, 1)

    def column(row_id, keep):
        dead = occ[pl.ds(row_id, 1), :].astype(F32)
        row = jnp.where((dead > 0.5) | jnp.logical_not(keep), NEG, 0.0)
        return jnp.broadcast_to(row, (BLOCK, BLOCK)).T

    for b in range(2):
        keep = fluid[dom * 2 + b] > 0
        bias[b, 0:128] = column(dom * 2, keep)
        bias[b, 128:256] = column(dom * 2 + 1, keep)
        bias[b, 256:384] = column(low_dom * 2 + low_ids[b], keep)
        bias[b, 384:512] = column(high_dom * 2 + high_ids[b], keep)

    def pair(p):
        lanes = pl.ds(pl.multiple_of(p * 128, 128), 128)
        q_t = (q[:, lanes].astype(F32) * SCALE).T.astype(BF16)
        q_cols = grouped_lanes(q_t)
        v_t = transposed(v[:, lanes])
        s_own = dot(k[:, lanes], q_cols)
        outs = []
        for b in range(2):
            k_n = neighbour_rows(k_low, k_high, low_ids, high_ids, b, lanes)
            v_n_t = transposed(neighbour_rows(v_low, v_high, low_ids, high_ids, b, lanes))
            s_n = dot(k_n, q_cols[:, 256 * b : 256 * b + 256])
            bias_o, bias_n = bias[b, 0:256], bias[b, 256:512]
            halves = []
            for h in range(2):
                g = 2 * b + h
                so = s_own[:, g * 128 : g * 128 + 128] + bias_o
                sn = s_n[:, h * 128 : h * 128 + 128] + bias_n
                m = jnp.maximum(
                    jnp.max(jnp.maximum(so, sn), axis=0, keepdims=True), 0.0
                )
                eo, en = jnp.exp(so - m), jnp.exp(sn - m)
                total = jnp.exp(-m) + jnp.sum(eo + en, axis=0, keepdims=True)
                inv = 1.0 / total
                po, pn = (eo * inv).astype(BF16), (en * inv).astype(BF16)
                probs[p, 0:256, g * 128 : g * 128 + 128] = po
                probs[p, 256:512, g * 128 : g * 128 + 128] = pn
                halves.append(
                    dot(v_t[h * HD : h * HD + HD], po) + dot(v_n_t[h * HD : h * HD + HD], pn)
                )
            outs.append(jnp.concatenate(halves, axis=0))
        out_t = jnp.concatenate(outs, axis=1)
        states_t[pl.ds(pl.multiple_of(p * 128, 128), 128), :] = out_t.astype(BF16)
        scratch[:, lanes] = out_t.T.astype(BF16)

    pl.loop(0, PAIRS, unroll=2)(pair)
    states[...] = scratch[...]
    for d, piece in ((1, p1), (2, p2), (3, p3)):
        start = pl.multiple_of(lax.rem(me + d, 4) * QUARTER, QUARTER)
        piece[...] = scratch[pl.ds(start, QUARTER), :]


def window_forward(place, lists, fluid, occ, q, k, v, k_low, v_low, k_high, v_high):
    piece = jax.ShapeDtypeStruct((QUARTER, D), BF16)
    return pl.pallas_call(
        forward_kernel,
        in_specs=[SMEM_SPEC] * 3 + [VMEM_SPEC] * 8,
        out_specs=[VMEM_SPEC] * 6,
        out_shape=[
            jax.ShapeDtypeStruct((TOK, D), BF16), piece, piece, piece,
            jax.ShapeDtypeStruct((PAIRS, 512, 512), BF16),
            jax.ShapeDtypeStruct((D, TOK), BF16),
        ],
        scratch_shapes=[pltpu.VMEM((2, 512, BLOCK), F32), pltpu.VMEM((TOK, D), BF16)],
        compiler_params=kernel_params(32),
        cost_estimate=cost(4_000_000_000, 16 << 20),
        name="window_forward",
    )(place, lists, fluid, occ, q, k, v, k_low, v_low, k_high, v_high)


ROWS = 16
WIDE = 256


def head_sums():
    row = lax.broadcasted_iota(jnp.int32, (2 * WIDE, WIDE), 0) % WIDE
    lane = lax.broadcasted_iota(jnp.int32, (2 * WIDE, WIDE), 1)
    return jnp.where(row // HD == lane // HD, 1.0, 0.0).astype(BF16)


def pair_sums(left, right, ones):
    products = jnp.concatenate([a * b for a in left for b in right], axis=0)
    high = products.astype(BF16)
    low = (products - high.astype(F32)).astype(BF16)
    sums = dot(jnp.concatenate([high, low], axis=1), ones)
    return [[sums[(4 * t + u) * ROWS : (4 * t + u + 1) * ROWS] for u in range(4)] for t in range(4)]


def time_first_kernel(place, q0, k0, g0, m1, m2, m3, s0, s1, s2, s3, attn, ones_ref):
    ones_ref[...] = head_sums()
    outs = (s0, s1, s2, s3)

    def tile(i):
        rows = pl.ds(pl.multiple_of((i // 4) * ROWS, ROWS), ROWS)
        lanes = pl.ds(pl.multiple_of((i % 4) * WIDE, WIDE), WIDE)
        qs = [x.astype(F32) for x in (q0[rows, lanes], *(m[0, rows, lanes] for m in (m1, m2, m3)))]
        ks = [x.astype(F32) for x in (k0[rows, lanes], *(m[1, rows, lanes] for m in (m1, m2, m3)))]
        gs = [x.astype(F32) for x in (g0[rows, lanes], *(m[2, rows, lanes] for m in (m1, m2, m3)))]
        scores = pair_sums([x * SCALE for x in qs], ks, ones_ref[...])
        sums = list(gs)
        for t in range(4):
            row = scores[t]
            top = jnp.maximum(jnp.maximum(row[0], row[1]), jnp.maximum(row[2], row[3]))
            exps = [jnp.exp(x - top) for x in row]
            inv = 1.0 / ((exps[0] + exps[1]) + (exps[2] + exps[3]))
            for u in range(4):
                a = exps[u] * inv
                attn[4 * t + u, rows, lanes] = a.astype(BF16)
                sums[u] = sums[u] + a * gs[t]
        for u in range(4):
            outs[u][rows, lanes] = sums[u].astype(BF16)

    pl.loop(0, 16)(tile)


def quarter_spec():
    return pl.BlockSpec((QUARTER, D), lambda i, s: (s[0], 0))


def whole_spec(*shape):
    return pl.BlockSpec(shape, lambda i, s: (0,) * len(shape))


def time_first(place, q, k, g, m1, m2, m3):
    piece = jax.ShapeDtypeStruct((QUARTER, D), BF16)
    return pl.pallas_call(
        time_first_kernel,
        grid_spec=pltpu.PrefetchScalarGridSpec(
            num_scalar_prefetch=1,
            grid=(1,),
            in_specs=[quarter_spec()] * 3 + [whole_spec(3, QUARTER, D)] * 3,
            out_specs=[whole_spec(QUARTER, D)] * 4 + [whole_spec(16, QUARTER, D)],
            scratch_shapes=[pltpu.VMEM((2 * WIDE, WIDE), BF16)],
        ),
        out_shape=[piece] * 4 + [jax.ShapeDtypeStruct((16, QUARTER, D), BF16)],
        compiler_params=kernel_params(24),
        cost_estimate=cost(1_000_000_000, 8 << 20),
        name="time_first",
    )(place, q, k, g, m1, m2, m3)


def time_second_kernel(
    place, q0, k0, g0, m1, m2, m3, attn, x0, x1, x2, x3, o0, o1, o2, o3, ones_ref
):
    ones_ref[...] = head_sums()
    outs = (o0, o1, o2, o3)

    def tile(i):
        rows = pl.ds(pl.multiple_of((i // 4) * ROWS, ROWS), ROWS)
        lanes = pl.ds(pl.multiple_of((i % 4) * WIDE, WIDE), WIDE)
        gs = [x.astype(F32) for x in (g0[rows, lanes], *(m[2, rows, lanes] for m in (m1, m2, m3)))]
        xs = [x[rows, lanes].astype(F32) for x in (x0, x1, x2, x3)]
        dattn = pair_sums(gs, xs, ones_ref[...])
        qs = [x.astype(F32) for x in (q0[rows, lanes], *(m[0, rows, lanes] for m in (m1, m2, m3)))]
        ks = [x.astype(F32) for x in (k0[rows, lanes], *(m[1, rows, lanes] for m in (m1, m2, m3)))]
        key_sums = [None] * 4
        for t in range(4):
            a = [attn[4 * t + u, rows, lanes].astype(F32) for u in range(4)]
            mean = sum(x * y for x, y in zip(a[1:], dattn[t][1:], strict=True)) + a[0] * dattn[t][0]
            query_sum = None
            for u in range(4):
                grad = a[u] * (dattn[t][u] - mean)
                query_sum = grad * ks[u] if query_sum is None else query_sum + grad * ks[u]
                term = grad * qs[t]
                key_sums[u] = term if key_sums[u] is None else key_sums[u] + term
            outs[t][0, rows, lanes] = (query_sum * SCALE).astype(BF16)
        for u in range(4):
            outs[u][1, rows, lanes] = (key_sums[u] * SCALE).astype(BF16)

    pl.loop(0, 16)(tile)


def time_second(place, q, k, g, m1, m2, m3, attn, states, x1, x2, x3):
    piece = jax.ShapeDtypeStruct((2, QUARTER, D), BF16)
    return pl.pallas_call(
        time_second_kernel,
        grid_spec=pltpu.PrefetchScalarGridSpec(
            num_scalar_prefetch=1,
            grid=(1,),
            in_specs=[quarter_spec()] * 3
            + [whole_spec(3, QUARTER, D)] * 3
            + [whole_spec(16, QUARTER, D), quarter_spec()]
            + [whole_spec(QUARTER, D)] * 3,
            out_specs=[whole_spec(2, QUARTER, D)] * 4,
            scratch_shapes=[pltpu.VMEM((2 * WIDE, WIDE), BF16)],
        ),
        out_shape=[piece] * 4,
        compiler_params=kernel_params(24),
        cost_estimate=cost(1_000_000_000, 8 << 20),
        name="time_second",
    )(place, q, k, g, m1, m2, m3, attn, states, x1, x2, x3)


def grad_rows(sg, place, pieces):
    for d, piece in enumerate(pieces):
        start = pl.multiple_of(lax.rem(place[0] + d, 4) * QUARTER, QUARTER)
        sg[pl.ds(start, QUARTER), :] = piece[...]


def deltas(sg_t, st_t):
    product = sg_t.astype(F32) * st_t.astype(F32)
    first = jnp.sum(product[:HD], axis=0, keepdims=True)
    second = jnp.sum(product[HD:], axis=0, keepdims=True)
    return jnp.concatenate(
        [first[:, :BLOCK], second[:, :BLOCK], first[:, BLOCK:], second[:, BLOCK:]], axis=1
    )


def back_sides_kernel(
    place, lists, q, k_low, v_low, k_high, v_high, probs, states_t, g0, g1, g2, g3,
    to_low, to_high, query_part, sg,
):
    low_ids, high_ids = listed(place, lists, 0), listed(place, lists, 1)
    grad_rows(sg, place, (g0, g1, g2, g3))

    def pair(p):
        lanes = pl.ds(pl.multiple_of(p * 128, 128), 128)
        rows = pl.ds(pl.multiple_of(p * 128, 128), 128)
        sg_p = sg[:, lanes]
        sg_t = transposed(sg_p)
        sg_cols, sg_rows, q_rows = grouped_lanes(sg_t), grouped_rows(sg_p), grouped_rows(q[:, lanes])
        delta = deltas(sg_t, states_t[rows, :])
        key_parts, value_parts = [], []
        for b in range(2):
            cols = slice(256 * b, 256 * b + 256)
            k_n = neighbour_rows(k_low, k_high, low_ids, high_ids, b, lanes)
            v_n = neighbour_rows(v_low, v_high, low_ids, high_ids, b, lanes)
            k_n_t = transposed(k_n)
            dp = dot(v_n, sg_cols[:, cols])
            pr = probs[p, 256:512, cols]
            ds = (pr.astype(F32) * (dp - delta[:, cols])).astype(BF16)
            query_part[rows, b * 128 : b * 128 + 128] = jnp.concatenate(
                [dot(k_n_t[:HD], ds[:, :BLOCK]), dot(k_n_t[HD:], ds[:, BLOCK:])], axis=0
            )
            key_parts.append(dot(ds, q_rows[cols]) * SCALE)
            value_parts.append(dot(pr, sg_rows[cols]))
        for n, parts in enumerate((key_parts, value_parts)):
            for ids, out, side in ((low_ids, to_low, 0), (high_ids, to_high, 1)):
                for j in range(2):
                    total = sum(
                        jnp.where(ids[b] == j, parts[b][side * 128 : side * 128 + 128], 0.0)
                        for b in range(2)
                    )
                    out[n, j * 128 : j * 128 + 128, lanes] = total.astype(BF16)

    pl.loop(0, PAIRS, unroll=2)(pair)


def back_sides(place, lists, q, k_low, v_low, k_high, v_high, probs, states_t, pieces):
    message = jax.ShapeDtypeStruct((2, TOK, D), BF16)
    return pl.pallas_call(
        back_sides_kernel,
        in_specs=[SMEM_SPEC] * 2 + [VMEM_SPEC] * 11,
        out_specs=[VMEM_SPEC] * 3,
        out_shape=[message, message, jax.ShapeDtypeStruct((D, TOK), F32)],
        scratch_shapes=[pltpu.VMEM((TOK, D), BF16)],
        compiler_params=kernel_params(32),
        cost_estimate=cost(6_000_000_000, 16 << 20),
        name="back_sides",
    )(place, lists, q, k_low, v_low, k_high, v_high, probs, states_t, *pieces)


def back_own_kernel(
    place, q, k, v, probs, states_t, query_part, g0, g1, g2, g3, query_grad, totals, sg
):
    grad_rows(sg, place, (g0, g1, g2, g3))

    def pair(p):
        lanes = pl.ds(pl.multiple_of(p * 128, 128), 128)
        rows = pl.ds(pl.multiple_of(p * 128, 128), 128)
        sg_p = sg[:, lanes]
        sg_t = transposed(sg_p)
        sg_cols, sg_rows, q_rows = grouped_lanes(sg_t), grouped_rows(sg_p), grouped_rows(q[:, lanes])
        delta = deltas(sg_t, states_t[rows, :])
        k_t = transposed(k[:, lanes])
        dp = dot(v[:, lanes], sg_cols)
        pr = probs[p, 0:256, :]
        ds = (pr.astype(F32) * (dp - delta)).astype(BF16)
        cols = [
            jnp.concatenate(
                [
                    dot(k_t[:HD], ds[:, 256 * b : 256 * b + 128]),
                    dot(k_t[HD:], ds[:, 256 * b + 128 : 256 * b + 256]),
                ],
                axis=0,
            )
            for b in range(2)
        ]
        query_t = jnp.concatenate(cols, axis=1) + query_part[rows, :]
        query_grad[:, lanes] = (query_t * SCALE).T.astype(BF16)
        totals[0, :, lanes] = dot(ds, q_rows) * SCALE
        totals[1, :, lanes] = dot(pr, sg_rows)

    pl.loop(0, PAIRS, unroll=2)(pair)


def back_own(place, q, k, v, probs, states_t, query_part, pieces):
    return pl.pallas_call(
        back_own_kernel,
        in_specs=[SMEM_SPEC] + [VMEM_SPEC] * 10,
        out_specs=[VMEM_SPEC] * 2,
        out_shape=[
            jax.ShapeDtypeStruct((TOK, D), BF16),
            jax.ShapeDtypeStruct((2, TOK, D), F32),
        ],
        scratch_shapes=[pltpu.VMEM((TOK, D), BF16)],
        compiler_params=kernel_params(32),
        cost_estimate=cost(6_000_000_000, 16 << 20),
        name="back_own",
    )(place, q, k, v, probs, states_t, query_part, *pieces)


def finish_kernel(place, totals, low, high, t0, t1, t2, t3, key_grad, value_grad, query_t, key_t):
    for n, out in ((0, key_grad), (1, value_grad)):
        out[...] = (totals[n] + low[n].astype(F32) + high[n].astype(F32)).astype(BF16)
    for d, piece in enumerate((t0, t1, t2, t3)):
        start = pl.multiple_of(lax.rem(place[0] + d, 4) * QUARTER, QUARTER)
        query_t[pl.ds(start, QUARTER), :] = piece[0]
        key_t[pl.ds(start, QUARTER), :] = piece[1]


def finish(place, totals, low, high, pieces):
    return pl.pallas_call(
        finish_kernel,
        in_specs=[SMEM_SPEC] + [VMEM_SPEC] * 7,
        out_specs=[VMEM_SPEC] * 4,
        out_shape=[jax.ShapeDtypeStruct((TOK, D), BF16)] * 4,
        compiler_params=kernel_params(24),
        cost_estimate=cost(0, 8 << 20),
        name="finish",
    )(place, totals, low, high, *pieces)


def body(
    queries, key_vectors, value_vectors, query_time, key_time, out_grad, fluid_mask, occupancy, key_lists
):
    q, k, v = queries[0], key_vectors[0], value_vectors[0]
    qt, kt, og = query_time[0], key_time[0], out_grad[0]
    me, dom = lax.axis_index("tm"), lax.axis_index("space")
    place = jnp.stack([me, dom]).astype(jnp.int32)
    lists = lax.dynamic_index_in_dim(key_lists, dom, 0, keepdims=False)[:, :, 1].reshape(-1)
    occ = occupancy.reshape(-1, BLOCK)

    domains, steps = lax.axis_size("space"), lax.axis_size("tm")
    up = [(i, (i + 1) % domains) for i in range(domains)]
    down = [(i, (i - 1) % domains) for i in range(domains)]

    def shift(x, d):
        return lax.ppermute(x, "tm", [(i, (i + d) % steps) for i in range(steps)])

    sent = stage(place, (qt, kt, og))
    arrived = {(4 - d) % 4: shift(sent[d - 1], d) for d in (1, 3, 2)}
    ms = (arrived[1], arrived[2], arrived[3])
    k_low, v_low = lax.ppermute(k, "space", up), lax.ppermute(v, "space", up)
    k_high, v_high = lax.ppermute(k, "space", down), lax.ppermute(v, "space", down)

    states, p1, p2, p3, probs, states_t = window_forward(
        place, lists, fluid_mask, occ, q, k, v, k_low, v_low, k_high, v_high
    )
    *grads, attn = time_first(place, qt, kt, og, *ms)
    home = {(4 - d) % 4: shift(grads[d], d) for d in (1, 3, 2)}
    grad_pieces = (grads[0], home[1], home[2], home[3])

    pieces = (None, p1, p2, p3)
    there = {(4 - d) % 4: shift(pieces[d], d) for d in (1, 3, 2)}
    back = time_second(place, qt, kt, og, *ms, attn, states, there[1], there[2], there[3])
    returned = {(4 - d) % 4: shift(back[d], d) for d in (1, 3, 2)}

    to_low, to_high, query_part = back_sides(
        place, lists, q, k_low, v_low, k_high, v_high, probs, states_t, grad_pieces
    )
    from_high = lax.ppermute(to_low, "space", down)
    from_low = lax.ppermute(to_high, "space", up)
    query_grad, totals = back_own(place, q, k, v, probs, states_t, query_part, grad_pieces)
    key_grad, value_grad, query_time_grad, key_time_grad = finish(
        place, totals, from_low, from_high, (back[0], returned[1], returned[2], returned[3])
    )
    return tuple(
        x[None] for x in (query_grad, key_grad, value_grad, query_time_grad, key_time_grad)
    )


def solution(mesh):
    split = P("tm", "space", None)
    return jax.shard_map(
        body,
        mesh=mesh,
        in_specs=(split,) * 6 + (P(),) * 3,
        out_specs=(split,) * 5,
        check_vma=False,
    )
```

```python
import functools

import jax
import jax.numpy as jnp
from jax import lax
from jax.experimental import pallas as pl
from jax.experimental.pallas import tpu as pltpu
from jax.sharding import PartitionSpec as P

BLOCK = 128
H = 16
HD = 64
D = 1024
TOK = 256
QUARTER = 64
PAIRS = 8
SCALE = HD**-0.5
NEG = -1e30
F32 = jnp.float32
BF16 = jnp.bfloat16

VMEM_SPEC = pl.BlockSpec(memory_space=pltpu.VMEM)
ANY_SPEC = pl.BlockSpec(memory_space=pl.ANY)
HBM_SPEC = pl.BlockSpec(memory_space=pltpu.MemorySpace.HBM)
SMEM_SPEC = pl.BlockSpec(memory_space=pltpu.SMEM)


def dot(a, b):
    return jnp.dot(a, b, preferred_element_type=F32)


def kernel_params(mib):
    return pltpu.CompilerParams(vmem_limit_bytes=mib * 1024 * 1024)


def cost(flops, nbytes):
    return pl.CostEstimate(flops=flops, bytes_accessed=nbytes, transcendentals=0)


def transposed(block):
    return block.astype(F32).T.astype(BF16)


def head_rows(block):
    row = lax.broadcasted_iota(jnp.int32, block.shape, 0)
    zero = jnp.zeros_like(block)
    return jnp.where(row < HD, block, zero), jnp.where(row < HD, zero, block)


def head_lanes(block):
    lane = lax.broadcasted_iota(jnp.int32, block.shape, 1)
    zero = jnp.zeros_like(block)
    return jnp.where(lane < HD, block, zero), jnp.where(lane < HD, zero, block)


def grouped_lanes(block_t):
    first, second = head_rows(block_t)
    return jnp.concatenate(
        [first[:, :BLOCK], second[:, :BLOCK], first[:, BLOCK:], second[:, BLOCK:]], axis=1
    )


def grouped_rows(block):
    first, second = head_lanes(block)
    return jnp.concatenate([first[:BLOCK], second[:BLOCK], first[BLOCK:], second[BLOCK:]], axis=0)


def stage_kernel(place, qt, kt, og, k, v, m1, m2, m3, kv, small, large, sems_in, sems_out):
    copies = []
    for d, out in ((1, m1), (3, m3), (2, m2)):
        start = pl.multiple_of(lax.rem(place[0] + d, 4) * QUARTER, QUARTER)
        for a, array in enumerate((qt, kt, og)):
            copies.append((array.at[pl.ds(start, QUARTER), :], small.at[3 * d - 3 + a], out.at[a]))
    copies += [(k, large.at[0], kv.at[0]), (v, large.at[1], kv.at[1])]
    ins = [pltpu.make_async_copy(a, b, sems_in.at[i]) for i, (a, b, c) in enumerate(copies)]
    outs = [pltpu.make_async_copy(b, c, sems_out.at[i]) for i, (a, b, c) in enumerate(copies)]
    for copy in ins:
        copy.start()
    for copy, after in zip(ins, outs, strict=True):
        copy.wait()
        after.start()
    for copy in outs:
        copy.wait()


def stage(place, *arrays):
    piece = jax.ShapeDtypeStruct((3, QUARTER, D), BF16)
    return pl.pallas_call(
        stage_kernel,
        in_specs=[SMEM_SPEC] + [HBM_SPEC] * 5,
        out_specs=[HBM_SPEC] * 4,
        out_shape=[piece] * 3 + [jax.ShapeDtypeStruct((2, TOK, D), BF16)],
        scratch_shapes=[
            pltpu.VMEM((9, QUARTER, D), BF16),
            pltpu.VMEM((2, TOK, D), BF16),
            pltpu.SemaphoreType.DMA((11,)),
            pltpu.SemaphoreType.DMA((11,)),
        ],
        compiler_params=kernel_params(60),
        cost_estimate=cost(0, 4 << 20),
        name="stage",
    )(place, *arrays)


def listed(place, lists, side):
    return [lists[b * 4 + 2 + side] for b in range(2)]


def neighbour_rows(low_ref, high_ref, low_ids, high_ids, b, lanes):
    low = low_ref[pl.ds(pl.multiple_of(low_ids[b] * BLOCK, BLOCK), BLOCK), lanes]
    high = high_ref[pl.ds(pl.multiple_of(high_ids[b] * BLOCK, BLOCK), BLOCK), lanes]
    return jnp.concatenate([low, high], axis=0)


def dead_column(occ, row_id, keep):
    dead = occ[pl.ds(row_id, 1), :].astype(F32)
    row = jnp.where((dead > 0.5) | jnp.logical_not(keep), NEG, 0.0)
    return jnp.broadcast_to(row, (BLOCK, BLOCK)).T


def pair_slice(p):
    return pl.ds(pl.multiple_of(p * 128, 128), 128)


def forward_own_kernel(place, fluid, occ, q, k, v, weights, stats, partial, bias):
    dom = place[1]
    for b in range(2):
        keep = fluid[dom * 2 + b] > 0
        for n in range(2):
            bias[b, n * 128 : n * 128 + 128] = dead_column(occ, dom * 2 + n, keep)

    def pair(p):
        lanes = pair_slice(p)
        q_cols = grouped_lanes((q[:, lanes].astype(F32) * SCALE).T.astype(BF16))
        v_t = transposed(v[:, lanes])
        scores = dot(k[:, lanes], q_cols)
        outs = []
        for g in range(4):
            cols = slice(g * 128, g * 128 + 128)
            s = scores[:, cols] + bias[g // 2]
            m = jnp.maximum(jnp.max(s, axis=0, keepdims=True), 0.0)
            e = jnp.exp(s - m)
            stats[p, 0:1, cols] = m
            stats[p, 1:2, cols] = jnp.sum(e, axis=0, keepdims=True)
            e = e.astype(BF16)
            weights[p, :, cols] = e
            outs.append(dot(v_t[(g % 2) * HD : (g % 2) * HD + HD], e))
        partial[pair_slice(p), :] = jnp.concatenate(
            [jnp.concatenate(outs[:2], axis=0), jnp.concatenate(outs[2:], axis=0)], axis=1
        )

    pl.loop(0, PAIRS, unroll=8)(pair)


def forward_own(place, fluid, occ, q, k, v):
    return pl.pallas_call(
        forward_own_kernel,
        in_specs=[SMEM_SPEC] * 2 + [VMEM_SPEC] * 4,
        out_specs=[VMEM_SPEC] * 3,
        out_shape=[
            jax.ShapeDtypeStruct((PAIRS, TOK, 512), BF16),
            jax.ShapeDtypeStruct((PAIRS, 8, 512), F32),
            jax.ShapeDtypeStruct((D, TOK), F32),
        ],
        scratch_shapes=[pltpu.VMEM((2, TOK, BLOCK), F32)],
        compiler_params=kernel_params(24),
        cost_estimate=cost(2_000_000_000, 8 << 20),
        name="forward_own",
    )(place, fluid, occ, q, k, v)


def forward_sides_kernel(
    place, lists, fluid, occ, q, low, high, stats, partial,
    states, p1, p2, p3, probs, states_t, factors, bias, scratch,
):
    me, dom = place[0], place[1]
    low_dom, high_dom = lax.rem(dom + 63, 64), lax.rem(dom + 1, 64)
    low_ids, high_ids = listed(place, lists, 0), listed(place, lists, 1)
    for b in range(2):
        keep = fluid[dom * 2 + b] > 0
        for h in (slice(0, 128), slice(128, 256)):
            bias[b, 0:128, h] = dead_column(occ, low_dom * 2 + low_ids[b], keep)
            bias[b, 128:256, h] = dead_column(occ, high_dom * 2 + high_ids[b], keep)

    def pair(p):
        lanes = pair_slice(p)
        q_cols = grouped_lanes((q[:, lanes].astype(F32) * SCALE).T.astype(BF16))
        outs = []
        for b in range(2):
            k_n = neighbour_rows(low.at[0], high.at[0], low_ids, high_ids, b, lanes)
            v_t = transposed(neighbour_rows(low.at[1], high.at[1], low_ids, high_ids, b, lanes))
            scores = dot(k_n, q_cols[:, 256 * b : 256 * b + 256])
            cols = slice(256 * b, 256 * b + 256)
            s = scores + bias[b]
            m_own, l_own = stats[p, 0:1, cols], stats[p, 1:2, cols]
            m = jnp.maximum(jnp.max(s, axis=0, keepdims=True), m_own)
            e = jnp.exp(s - m)
            scale_own = jnp.exp(m_own - m)
            total = jnp.exp(-m) + scale_own * l_own + jnp.sum(e, axis=0, keepdims=True)
            inv = 1.0 / total
            own = scale_own * inv
            factors[p, 0:1, cols] = own
            pr = (e * inv).astype(BF16)
            probs[p, :, cols] = pr
            halves = []
            for h in range(2):
                rows = pl.ds(pl.multiple_of(p * 128 + h * HD, HD), HD)
                half = slice(h * 128, h * 128 + 128)
                halves.append(
                    dot(v_t[h * HD : h * HD + HD], pr[:, half])
                    + partial[rows, b * 128 : b * 128 + 128] * own[:, half]
                )
            outs.append(jnp.concatenate(halves, axis=0))
        out_t = jnp.concatenate(outs, axis=1)
        states_t[pair_slice(p), :] = out_t.astype(BF16)
        scratch[:, lanes] = out_t.T.astype(BF16)

    pl.loop(0, PAIRS, unroll=8)(pair)
    for d, piece in ((0, states), (1, p1), (2, p2), (3, p3)):
        start = pl.multiple_of(lax.rem(me + d, 4) * QUARTER, QUARTER)
        piece[...] = scratch[pl.ds(start, QUARTER), :]


def forward_sides(place, lists, fluid, occ, q, low, high, stats, partial):
    piece = jax.ShapeDtypeStruct((QUARTER, D), BF16)
    return pl.pallas_call(
        forward_sides_kernel,
        in_specs=[SMEM_SPEC] * 3 + [VMEM_SPEC] * 6,
        out_specs=[VMEM_SPEC] * 7,
        out_shape=[piece] * 4
        + [
            jax.ShapeDtypeStruct((PAIRS, TOK, 512), BF16),
            jax.ShapeDtypeStruct((D, TOK), BF16),
            jax.ShapeDtypeStruct((PAIRS, 8, 512), F32),
        ],
        scratch_shapes=[pltpu.VMEM((2, TOK, TOK), F32), pltpu.VMEM((TOK, D), BF16)],
        compiler_params=kernel_params(24),
        cost_estimate=cost(2_000_000_000, 8 << 20),
        name="forward_sides",
    )(place, lists, fluid, occ, q, low, high, stats, partial)


ROWS = 16
WIDE = 256


def head_sums():
    row = lax.broadcasted_iota(jnp.int32, (2 * WIDE, WIDE), 0) % WIDE
    lane = lax.broadcasted_iota(jnp.int32, (2 * WIDE, WIDE), 1)
    return jnp.where(row // HD == lane // HD, 1.0, 0.0).astype(BF16)


def pair_sums(left, right, ones):
    products = jnp.concatenate([a * b for a in left for b in right], axis=0)
    high = products.astype(BF16)
    low = (products - high.astype(F32)).astype(BF16)
    sums = dot(jnp.concatenate([high, low], axis=1), ones)
    return [[sums[(4 * t + u) * ROWS : (4 * t + u + 1) * ROWS] for u in range(4)] for t in range(4)]


def time_first_kernel(place, q0, k0, g0, m1, m2, m3, after, s0, s1, s2, s3, attn, ones_ref):
    ones_ref[...] = head_sums()
    outs = (s0, s1, s2, s3)

    def tile(i):
        rows = pl.ds(pl.multiple_of((i // 4) * ROWS, ROWS), ROWS)
        lanes = pl.ds(pl.multiple_of((i % 4) * WIDE, WIDE), WIDE)
        here = pl.ds(pl.multiple_of(place[0] * QUARTER + (i // 4) * ROWS, ROWS), ROWS)
        qs = [x.astype(F32) for x in (q0[here, lanes], *(m[0, rows, lanes] for m in (m1, m2, m3)))]
        ks = [x.astype(F32) for x in (k0[here, lanes], *(m[1, rows, lanes] for m in (m1, m2, m3)))]
        gs = [x.astype(F32) for x in (g0[here, lanes], *(m[2, rows, lanes] for m in (m1, m2, m3)))]
        scores = pair_sums([x * SCALE for x in qs], ks, ones_ref[...])
        sums = list(gs)
        for t in range(4):
            row = scores[t]
            top = jnp.maximum(jnp.maximum(row[0], row[1]), jnp.maximum(row[2], row[3]))
            exps = [jnp.exp(x - top) for x in row]
            inv = 1.0 / ((exps[0] + exps[1]) + (exps[2] + exps[3]))
            for u in range(4):
                a = exps[u] * inv
                attn[4 * t + u, rows, lanes] = a.astype(BF16)
                sums[u] = sums[u] + a * gs[t]
        for u in range(4):
            outs[u][rows, lanes] = sums[u].astype(BF16)

    pl.loop(0, 16, unroll=4)(tile)


def time_first(place, q, k, g, m1, m2, m3, after):
    piece = jax.ShapeDtypeStruct((QUARTER, D), BF16)
    return pl.pallas_call(
        time_first_kernel,
        in_specs=[SMEM_SPEC] + [VMEM_SPEC] * 6 + [ANY_SPEC],
        out_specs=[VMEM_SPEC] * 5,
        out_shape=[piece] * 4 + [jax.ShapeDtypeStruct((16, QUARTER, D), BF16)],
        scratch_shapes=[pltpu.VMEM((2 * WIDE, WIDE), BF16)],
        compiler_params=kernel_params(24),
        cost_estimate=cost(1_000_000_000, 8 << 20),
        name="time_first",
    )(place, q, k, g, m1, m2, m3, after)


def time_second_kernel(
    place, q0, k0, g0, m1, m2, m3, attn, x0, x1, x2, x3, o0, o1, o2, o3, ones_ref
):
    ones_ref[...] = head_sums()
    outs = (o0, o1, o2, o3)

    def tile(i):
        rows = pl.ds(pl.multiple_of((i // 4) * ROWS, ROWS), ROWS)
        lanes = pl.ds(pl.multiple_of((i % 4) * WIDE, WIDE), WIDE)
        here = pl.ds(pl.multiple_of(place[0] * QUARTER + (i // 4) * ROWS, ROWS), ROWS)
        gs = [x.astype(F32) for x in (g0[here, lanes], *(m[2, rows, lanes] for m in (m1, m2, m3)))]
        xs = [x[rows, lanes].astype(F32) for x in (x0, x1, x2, x3)]
        dattn = pair_sums(gs, xs, ones_ref[...])
        qs = [x.astype(F32) for x in (q0[here, lanes], *(m[0, rows, lanes] for m in (m1, m2, m3)))]
        ks = [x.astype(F32) for x in (k0[here, lanes], *(m[1, rows, lanes] for m in (m1, m2, m3)))]
        key_sums = [None] * 4
        for t in range(4):
            a = [attn[4 * t + u, rows, lanes].astype(F32) for u in range(4)]
            mean = sum(x * y for x, y in zip(a[1:], dattn[t][1:], strict=True)) + a[0] * dattn[t][0]
            query_sum = None
            for u in range(4):
                grad = a[u] * (dattn[t][u] - mean)
                query_sum = grad * ks[u] if query_sum is None else query_sum + grad * ks[u]
                term = grad * qs[t]
                key_sums[u] = term if key_sums[u] is None else key_sums[u] + term
            outs[t][0, rows, lanes] = (query_sum * SCALE).astype(BF16)
        for u in range(4):
            outs[u][1, rows, lanes] = (key_sums[u] * SCALE).astype(BF16)

    pl.loop(0, 16, unroll=4)(tile)


def time_second(place, q, k, g, m1, m2, m3, attn, x0, x1, x2, x3):
    piece = jax.ShapeDtypeStruct((2, QUARTER, D), BF16)
    return pl.pallas_call(
        time_second_kernel,
        in_specs=[SMEM_SPEC] + [VMEM_SPEC] * 11,
        out_specs=[VMEM_SPEC] * 4,
        out_shape=[piece] * 4,
        scratch_shapes=[pltpu.VMEM((2 * WIDE, WIDE), BF16)],
        compiler_params=kernel_params(24),
        cost_estimate=cost(1_000_000_000, 8 << 20),
        name="time_second",
    )(place, q, k, g, m1, m2, m3, attn, x0, x1, x2, x3)


def grad_rows(sg, place, pieces):
    for d, piece in enumerate(pieces):
        start = pl.multiple_of(lax.rem(place[0] + d, 4) * QUARTER, QUARTER)
        sg[pl.ds(start, QUARTER), :] = piece[...]


def deltas(sg_t, st_t):
    product = sg_t.astype(F32) * st_t.astype(F32)
    first = jnp.sum(product[:HD], axis=0, keepdims=True)
    second = jnp.sum(product[HD:], axis=0, keepdims=True)
    return jnp.concatenate(
        [first[:, :BLOCK], second[:, :BLOCK], first[:, BLOCK:], second[:, BLOCK:]], axis=1
    )


def back_sides_kernel(
    place, lists, q, from_low, from_high, probs, states_t, g0, g1, g2, g3, after,
    to_low, to_high, query_part, sg,
):
    low_ids, high_ids = listed(place, lists, 0), listed(place, lists, 1)
    grad_rows(sg, place, (g0, g1, g2, g3))

    def pair(p):
        lanes = pl.ds(pl.multiple_of(p * 128, 128), 128)
        rows = pl.ds(pl.multiple_of(p * 128, 128), 128)
        sg_p = sg[:, lanes]
        sg_t = transposed(sg_p)
        sg_cols, sg_rows, q_rows = grouped_lanes(sg_t), grouped_rows(sg_p), grouped_rows(q[:, lanes])
        delta = deltas(sg_t, states_t[rows, :])
        key_parts, value_parts = [], []
        for b in range(2):
            cols = slice(256 * b, 256 * b + 256)
            k_n = neighbour_rows(from_low.at[0], from_high.at[0], low_ids, high_ids, b, lanes)
            v_n = neighbour_rows(from_low.at[1], from_high.at[1], low_ids, high_ids, b, lanes)
            k_n_t = transposed(k_n)
            dp = dot(v_n, sg_cols[:, cols])
            pr = probs[p, :, cols]
            ds = (pr.astype(F32) * (dp - delta[:, cols])).astype(BF16)
            query_part[rows, b * 128 : b * 128 + 128] = jnp.concatenate(
                [dot(k_n_t[:HD], ds[:, :BLOCK]), dot(k_n_t[HD:], ds[:, BLOCK:])], axis=0
            )
            key_parts.append(dot(ds, q_rows[cols]) * SCALE)
            value_parts.append(dot(pr, sg_rows[cols]))
        for n, parts in enumerate((key_parts, value_parts)):
            for ids, out, side in ((low_ids, to_low, 0), (high_ids, to_high, 1)):
                for j in range(2):
                    total = sum(
                        jnp.where(ids[b] == j, parts[b][side * 128 : side * 128 + 128], 0.0)
                        for b in range(2)
                    )
                    out[n, j * 128 : j * 128 + 128, lanes] = total.astype(BF16)

    pl.loop(0, PAIRS, unroll=8)(pair)


def back_sides(place, lists, q, low, high, probs, states_t, pieces, after):
    message = jax.ShapeDtypeStruct((2, TOK, D), BF16)
    return pl.pallas_call(
        back_sides_kernel,
        in_specs=[SMEM_SPEC] * 2 + [VMEM_SPEC] * 9 + [ANY_SPEC],
        out_specs=[VMEM_SPEC] * 3,
        out_shape=[message, message, jax.ShapeDtypeStruct((D, TOK), F32)],
        scratch_shapes=[pltpu.VMEM((TOK, D), BF16)],
        compiler_params=kernel_params(32),
        cost_estimate=cost(6_000_000_000, 16 << 20),
        name="back_sides",
    )(place, lists, q, low, high, probs, states_t, *pieces, after)


def back_own_kernel(
    place, q, k, v, weights, factors, states_t, query_part, g0, g1, g2, g3, query_grad, totals, sg
):
    grad_rows(sg, place, (g0, g1, g2, g3))

    def pair(p):
        lanes = pl.ds(pl.multiple_of(p * 128, 128), 128)
        rows = pl.ds(pl.multiple_of(p * 128, 128), 128)
        sg_p = sg[:, lanes]
        sg_t = transposed(sg_p)
        q_rows = grouped_rows(q[:, lanes])
        factor = factors[p, 0:1, :]
        delta = deltas(sg_t, states_t[rows, :]) * factor
        scaled = grouped_lanes(sg_t).astype(F32) * factor
        sg_cols, sg_rows = scaled.astype(BF16), scaled.T.astype(BF16)
        k_t = transposed(k[:, lanes])
        dp = dot(v[:, lanes], sg_cols)
        pr = weights[p]
        ds = (pr.astype(F32) * (dp - delta)).astype(BF16)
        cols = [
            jnp.concatenate(
                [
                    dot(k_t[:HD], ds[:, 256 * b : 256 * b + 128]),
                    dot(k_t[HD:], ds[:, 256 * b + 128 : 256 * b + 256]),
                ],
                axis=0,
            )
            for b in range(2)
        ]
        query_t = jnp.concatenate(cols, axis=1) + query_part[rows, :]
        query_grad[:, lanes] = (query_t * SCALE).T.astype(BF16)
        totals[0, :, lanes] = dot(ds, q_rows) * SCALE
        totals[1, :, lanes] = dot(pr, sg_rows)

    pl.loop(0, PAIRS, unroll=8)(pair)


def back_own(place, q, k, v, weights, factors, states_t, query_part, pieces):
    return pl.pallas_call(
        back_own_kernel,
        in_specs=[SMEM_SPEC] + [VMEM_SPEC] * 11,
        out_specs=[VMEM_SPEC] * 2,
        out_shape=[
            jax.ShapeDtypeStruct((TOK, D), BF16),
            jax.ShapeDtypeStruct((2, TOK, D), F32),
        ],
        scratch_shapes=[pltpu.VMEM((TOK, D), BF16)],
        compiler_params=kernel_params(32),
        cost_estimate=cost(6_000_000_000, 16 << 20),
        name="back_own",
    )(place, q, k, v, weights, factors, states_t, query_part, *pieces)


def finish_time_kernel(place, t0, t1, t2, t3, query_t, key_t):
    for d, piece in enumerate((t0, t1, t2, t3)):
        start = pl.multiple_of(lax.rem(place[0] + d, 4) * QUARTER, QUARTER)
        query_t[pl.ds(start, QUARTER), :] = piece[0]
        key_t[pl.ds(start, QUARTER), :] = piece[1]


def finish_time(place, pieces):
    return pl.pallas_call(
        finish_time_kernel,
        in_specs=[SMEM_SPEC] + [VMEM_SPEC] * 4,
        out_specs=[VMEM_SPEC] * 2,
        out_shape=[jax.ShapeDtypeStruct((TOK, D), BF16)] * 2,
        compiler_params=kernel_params(24),
        cost_estimate=cost(0, 2 << 20),
        name="finish_time",
    )(place, *pieces)


def finish_kernel(totals, low, high, key_grad, value_grad):
    for n, out in ((0, key_grad), (1, value_grad)):
        out[...] = (totals[n] + low[n].astype(F32) + high[n].astype(F32)).astype(BF16)


def finish(totals, low, high):
    return pl.pallas_call(
        finish_kernel,
        in_specs=[VMEM_SPEC] * 3,
        out_specs=[VMEM_SPEC] * 2,
        out_shape=[jax.ShapeDtypeStruct((TOK, D), BF16)] * 2,
        compiler_params=kernel_params(24),
        cost_estimate=cost(0, 5 << 20),
        name="finish",
    )(totals, low, high)


def body(
    queries, key_vectors, value_vectors, query_time, key_time, out_grad, fluid_mask, occupancy, key_lists
):
    q, k, v = queries[0], key_vectors[0], value_vectors[0]
    qt, kt, og = query_time[0], key_time[0], out_grad[0]
    me, dom = lax.axis_index("tm"), lax.axis_index("space")
    place = jnp.stack([me, dom]).astype(jnp.int32)
    lists = lax.dynamic_index_in_dim(key_lists, dom, 0, keepdims=False)[:, :, 1].reshape(-1)
    occ = occupancy.reshape(-1, BLOCK)

    domains, steps = lax.axis_size("space"), lax.axis_size("tm")
    up = [(i, (i + 1) % domains) for i in range(domains)]
    down = [(i, (i - 1) % domains) for i in range(domains)]

    def shift(x, d):
        return lax.ppermute(x, "tm", [(i, (i + d) % steps) for i in range(steps)])

    m1, m2, m3, kv = stage(place, qt, kt, og, k, v)
    sent = (None, m1, m2, m3)
    arrived = {(4 - d) % 4: shift(sent[d], d) for d in (1, 3, 2)}
    ms = (arrived[1], arrived[2], arrived[3])
    low, high = lax.ppermute(kv, "space", up), lax.ppermute(kv, "space", down)

    weights, stats, partial = forward_own(place, fluid_mask, occ, q, k, v)
    *pieces, probs, states_t, factors = forward_sides(
        place, lists, fluid_mask, occ, q, low, high, stats, partial
    )
    *grads, attn = time_first(place, qt, kt, og, *ms, pieces[0])
    home = {(4 - d) % 4: shift(grads[d], d) for d in (1, 3, 2)}
    grad_pieces = (grads[0], home[1], home[2], home[3])

    there = {(4 - d) % 4: shift(pieces[d], d) for d in (1, 3, 2)}
    back = time_second(place, qt, kt, og, *ms, attn, pieces[0], there[1], there[2], there[3])

    to_low, to_high, query_part = back_sides(
        place, lists, q, low, high, probs, states_t, grad_pieces, back[0]
    )
    from_high = lax.ppermute(to_low, "space", down)
    from_low = lax.ppermute(to_high, "space", up)
    returned = {(4 - d) % 4: shift(back[d], d) for d in (1, 3, 2)}
    query_time_grad, key_time_grad = finish_time(
        place, (back[0], returned[1], returned[2], returned[3])
    )
    query_grad, totals = back_own(
        place, q, k, v, weights, factors, states_t, query_part, grad_pieces
    )
    key_grad, value_grad = finish(totals, from_low, from_high)
    return tuple(
        x[None] for x in (query_grad, key_grad, value_grad, query_time_grad, key_time_grad)
    )


def solution(mesh):
    split = P("tm", "space", None)
    return jax.shard_map(
        body,
        mesh=mesh,
        in_specs=(split,) * 6 + (P(),) * 3,
        out_specs=(split,) * 5,
        check_vma=False,
    )
```

```python
import functools

import jax
import jax.numpy as jnp
from jax import lax
from jax.experimental import pallas as pl
from jax.experimental.pallas import tpu as pltpu
from jax.sharding import PartitionSpec as P

BLOCK = 128
H = 16
HD = 64
D = 1024
TOK = 256
QUARTER = 64
PAIRS = 8
SCALE = HD**-0.5
NEG = -1e30
F32 = jnp.float32
BF16 = jnp.bfloat16

VMEM_SPEC = pl.BlockSpec(memory_space=pltpu.VMEM)
ANY_SPEC = pl.BlockSpec(memory_space=pl.ANY)
HBM_SPEC = pl.BlockSpec(memory_space=pltpu.MemorySpace.HBM)
SMEM_SPEC = pl.BlockSpec(memory_space=pltpu.SMEM)


def dot(a, b):
    return jnp.dot(a, b, preferred_element_type=F32)


def dot_t(a, b):
    return lax.dot_general(a, b, (((1,), (1,)), ((), ())), preferred_element_type=F32)


def kernel_params(mib):
    return pltpu.CompilerParams(vmem_limit_bytes=mib * 1024 * 1024)


def cost(flops, nbytes):
    return pl.CostEstimate(flops=flops, bytes_accessed=nbytes, transcendentals=0)


def transposed(block):
    return block.astype(F32).T.astype(BF16)


def head_rows(block):
    row = lax.broadcasted_iota(jnp.int32, block.shape, 0)
    zero = jnp.zeros_like(block)
    return jnp.where(row < HD, block, zero), jnp.where(row < HD, zero, block)


def head_lanes(block):
    lane = lax.broadcasted_iota(jnp.int32, block.shape, 1)
    zero = jnp.zeros_like(block)
    return jnp.where(lane < HD, block, zero), jnp.where(lane < HD, zero, block)


def grouped_lanes(block_t):
    first, second = head_rows(block_t)
    return jnp.concatenate(
        [first[:, :BLOCK], second[:, :BLOCK], first[:, BLOCK:], second[:, BLOCK:]], axis=1
    )


def grouped_rows(block):
    first, second = head_lanes(block)
    return jnp.concatenate([first[:BLOCK], second[:BLOCK], first[BLOCK:], second[BLOCK:]], axis=0)


def stage_kernel(place, qt, kt, og, k, v, m1, m2, m3, kv, small, large, sems_in, sems_out):
    copies = []
    for d, out in ((1, m1), (3, m3), (2, m2)):
        start = pl.multiple_of(lax.rem(place[0] + d, 4) * QUARTER, QUARTER)
        for a, array in enumerate((qt, kt, og)):
            copies.append((array.at[pl.ds(start, QUARTER), :], small.at[3 * d - 3 + a], out.at[a]))
    copies += [(k, large.at[0], kv.at[0]), (v, large.at[1], kv.at[1])]
    ins = [pltpu.make_async_copy(a, b, sems_in.at[i]) for i, (a, b, c) in enumerate(copies)]
    outs = [pltpu.make_async_copy(b, c, sems_out.at[i]) for i, (a, b, c) in enumerate(copies)]
    for copy in ins:
        copy.start()
    for copy, after in zip(ins, outs, strict=True):
        copy.wait()
        after.start()
    for copy in outs:
        copy.wait()


def stage(place, *arrays):
    piece = jax.ShapeDtypeStruct((3, QUARTER, D), BF16)
    return pl.pallas_call(
        stage_kernel,
        in_specs=[SMEM_SPEC] + [HBM_SPEC] * 5,
        out_specs=[HBM_SPEC] * 4,
        out_shape=[piece] * 3 + [jax.ShapeDtypeStruct((2, TOK, D), BF16)],
        scratch_shapes=[
            pltpu.VMEM((9, QUARTER, D), BF16),
            pltpu.VMEM((2, TOK, D), BF16),
            pltpu.SemaphoreType.DMA((11,)),
            pltpu.SemaphoreType.DMA((11,)),
        ],
        compiler_params=kernel_params(60),
        cost_estimate=cost(0, 4 << 20),
        name="stage",
    )(place, *arrays)


def listed(place, lists, side):
    return [lists[b * 4 + 2 + side] for b in range(2)]


def neighbour_rows(low_ref, high_ref, low_ids, high_ids, b, lanes):
    low = low_ref[pl.ds(pl.multiple_of(low_ids[b] * BLOCK, BLOCK), BLOCK), lanes]
    high = high_ref[pl.ds(pl.multiple_of(high_ids[b] * BLOCK, BLOCK), BLOCK), lanes]
    return jnp.concatenate([low, high], axis=0)


def dead_column(occ, row_id, keep):
    dead = occ[pl.ds(row_id, 1), :].astype(F32)
    row = jnp.where((dead > 0.5) | jnp.logical_not(keep), NEG, 0.0)
    return jnp.broadcast_to(row, (BLOCK, BLOCK)).T


def pair_slice(p):
    return pl.ds(pl.multiple_of(p * 128, 128), 128)


def forward_own_kernel(place, fluid, occ, q, k, v, weights, stats, partial, bias):
    dom = place[1]
    for b in range(2):
        keep = fluid[dom * 2 + b] > 0
        for n in range(2):
            bias[b, n * 128 : n * 128 + 128] = dead_column(occ, dom * 2 + n, keep)

    def pair(p):
        lanes = pair_slice(p)
        q_cols = grouped_lanes((q[:, lanes].astype(F32) * SCALE).T.astype(BF16))
        v_t = transposed(v[:, lanes])
        scores = dot(k[:, lanes], q_cols)
        outs = []
        for g in range(4):
            cols = slice(g * 128, g * 128 + 128)
            s = scores[:, cols] + bias[g // 2]
            m = jnp.maximum(jnp.max(s, axis=0, keepdims=True), 0.0)
            e = jnp.exp(s - m)
            stats[p, 0:1, cols] = m
            stats[p, 1:2, cols] = jnp.sum(e, axis=0, keepdims=True)
            e = e.astype(BF16)
            weights[p, :, cols] = e
            outs.append(dot(v_t[(g % 2) * HD : (g % 2) * HD + HD], e))
        partial[pair_slice(p), :] = jnp.concatenate(
            [jnp.concatenate(outs[:2], axis=0), jnp.concatenate(outs[2:], axis=0)], axis=1
        )

    pl.loop(0, PAIRS, unroll=8)(pair)


def forward_own(place, fluid, occ, q, k, v):
    return pl.pallas_call(
        forward_own_kernel,
        in_specs=[SMEM_SPEC] * 2 + [VMEM_SPEC] * 4,
        out_specs=[VMEM_SPEC] * 3,
        out_shape=[
            jax.ShapeDtypeStruct((PAIRS, TOK, 512), BF16),
            jax.ShapeDtypeStruct((PAIRS, 8, 512), F32),
            jax.ShapeDtypeStruct((D, TOK), F32),
        ],
        scratch_shapes=[pltpu.VMEM((2, TOK, BLOCK), F32)],
        compiler_params=kernel_params(24),
        cost_estimate=cost(2_000_000_000, 8 << 20),
        name="forward_own",
    )(place, fluid, occ, q, k, v)


def forward_sides_kernel(
    place, lists, fluid, occ, q, low, high, stats, partial,
    states, p1, p2, p3, probs, states_t, factors, bias, scratch,
):
    me, dom = place[0], place[1]
    low_dom, high_dom = lax.rem(dom + 63, 64), lax.rem(dom + 1, 64)
    low_ids, high_ids = listed(place, lists, 0), listed(place, lists, 1)
    for b in range(2):
        keep = fluid[dom * 2 + b] > 0
        for h in (slice(0, 128), slice(128, 256)):
            bias[b, 0:128, h] = dead_column(occ, low_dom * 2 + low_ids[b], keep)
            bias[b, 128:256, h] = dead_column(occ, high_dom * 2 + high_ids[b], keep)

    def pair(p):
        lanes = pair_slice(p)
        q_cols = grouped_lanes((q[:, lanes].astype(F32) * SCALE).T.astype(BF16))
        outs = []
        for b in range(2):
            k_n = neighbour_rows(low.at[0], high.at[0], low_ids, high_ids, b, lanes)
            v_t = transposed(neighbour_rows(low.at[1], high.at[1], low_ids, high_ids, b, lanes))
            scores = dot(k_n, q_cols[:, 256 * b : 256 * b + 256])
            cols = slice(256 * b, 256 * b + 256)
            s = scores + bias[b]
            m_own, l_own = stats[p, 0:1, cols], stats[p, 1:2, cols]
            m = jnp.maximum(jnp.max(s, axis=0, keepdims=True), m_own)
            e = jnp.exp(s - m)
            scale_own = jnp.exp(m_own - m)
            total = jnp.exp(-m) + scale_own * l_own + jnp.sum(e, axis=0, keepdims=True)
            inv = 1.0 / total
            own = scale_own * inv
            factors[p, 0:1, cols] = own
            pr = (e * inv).astype(BF16)
            probs[p, :, cols] = pr
            halves = []
            for h in range(2):
                rows = pl.ds(pl.multiple_of(p * 128 + h * HD, HD), HD)
                half = slice(h * 128, h * 128 + 128)
                halves.append(
                    dot(v_t[h * HD : h * HD + HD], pr[:, half])
                    + partial[rows, b * 128 : b * 128 + 128] * own[:, half]
                )
            outs.append(jnp.concatenate(halves, axis=0))
        out_t = jnp.concatenate(outs, axis=1)
        states_t[pair_slice(p), :] = out_t.astype(BF16)
        scratch[:, lanes] = out_t.T.astype(BF16)

    pl.loop(0, PAIRS, unroll=8)(pair)
    for d, piece in ((0, states), (1, p1), (2, p2), (3, p3)):
        start = pl.multiple_of(lax.rem(me + d, 4) * QUARTER, QUARTER)
        piece[...] = scratch[pl.ds(start, QUARTER), :]


def forward_sides(place, lists, fluid, occ, q, low, high, stats, partial):
    piece = jax.ShapeDtypeStruct((QUARTER, D), BF16)
    return pl.pallas_call(
        forward_sides_kernel,
        in_specs=[SMEM_SPEC] * 3 + [VMEM_SPEC] * 6,
        out_specs=[VMEM_SPEC] * 7,
        out_shape=[piece] * 4
        + [
            jax.ShapeDtypeStruct((PAIRS, TOK, 512), BF16),
            jax.ShapeDtypeStruct((D, TOK), BF16),
            jax.ShapeDtypeStruct((PAIRS, 8, 512), F32),
        ],
        scratch_shapes=[pltpu.VMEM((2, TOK, TOK), F32), pltpu.VMEM((TOK, D), BF16)],
        compiler_params=kernel_params(24),
        cost_estimate=cost(2_000_000_000, 8 << 20),
        name="forward_sides",
    )(place, lists, fluid, occ, q, low, high, stats, partial)


ROWS = 16
WIDE = 256


def head_sums():
    row = lax.broadcasted_iota(jnp.int32, (2 * WIDE, WIDE), 0) % WIDE
    lane = lax.broadcasted_iota(jnp.int32, (2 * WIDE, WIDE), 1)
    return jnp.where(row // HD == lane // HD, 1.0, 0.0).astype(BF16)


def pair_sums(left, right, ones):
    products = jnp.concatenate([a * b for a in left for b in right], axis=0)
    high = products.astype(BF16)
    low = (products - high.astype(F32)).astype(BF16)
    sums = dot(jnp.concatenate([high, low], axis=1), ones)
    return [[sums[(4 * t + u) * ROWS : (4 * t + u + 1) * ROWS] for u in range(4)] for t in range(4)]


def time_first_kernel(place, q0, k0, g0, m1, m2, m3, after, s0, s1, s2, s3, attn, ones_ref):
    ones_ref[...] = head_sums()
    outs = (s0, s1, s2, s3)

    def tile(i):
        rows = pl.ds(pl.multiple_of((i // 4) * ROWS, ROWS), ROWS)
        lanes = pl.ds(pl.multiple_of((i % 4) * WIDE, WIDE), WIDE)
        here = pl.ds(pl.multiple_of(place[0] * QUARTER + (i // 4) * ROWS, ROWS), ROWS)
        qs = [x.astype(F32) for x in (q0[here, lanes], *(m[0, rows, lanes] for m in (m1, m2, m3)))]
        ks = [x.astype(F32) for x in (k0[here, lanes], *(m[1, rows, lanes] for m in (m1, m2, m3)))]
        gs = [x.astype(F32) for x in (g0[here, lanes], *(m[2, rows, lanes] for m in (m1, m2, m3)))]
        scores = pair_sums([x * SCALE for x in qs], ks, ones_ref[...])
        sums = list(gs)
        for t in range(4):
            row = scores[t]
            top = jnp.maximum(jnp.maximum(row[0], row[1]), jnp.maximum(row[2], row[3]))
            exps = [jnp.exp(x - top) for x in row]
            inv = 1.0 / ((exps[0] + exps[1]) + (exps[2] + exps[3]))
            for u in range(4):
                a = exps[u] * inv
                attn[4 * t + u, rows, lanes] = a.astype(BF16)
                sums[u] = sums[u] + a * gs[t]
        for u in range(4):
            outs[u][rows, lanes] = sums[u].astype(BF16)

    pl.loop(0, 16, unroll=4)(tile)


def time_first(place, q, k, g, m1, m2, m3, after):
    piece = jax.ShapeDtypeStruct((QUARTER, D), BF16)
    return pl.pallas_call(
        time_first_kernel,
        in_specs=[SMEM_SPEC] + [VMEM_SPEC] * 6 + [ANY_SPEC],
        out_specs=[VMEM_SPEC] * 5,
        out_shape=[piece] * 4 + [jax.ShapeDtypeStruct((16, QUARTER, D), BF16)],
        scratch_shapes=[pltpu.VMEM((2 * WIDE, WIDE), BF16)],
        compiler_params=kernel_params(24),
        cost_estimate=cost(1_000_000_000, 8 << 20),
        name="time_first",
    )(place, q, k, g, m1, m2, m3, after)


def time_second_kernel(
    place, q0, k0, g0, m1, m2, m3, attn, x0, x1, x2, x3, o0, o1, o2, o3, ones_ref
):
    ones_ref[...] = head_sums()
    outs = (o0, o1, o2, o3)

    def tile(i):
        rows = pl.ds(pl.multiple_of((i // 4) * ROWS, ROWS), ROWS)
        lanes = pl.ds(pl.multiple_of((i % 4) * WIDE, WIDE), WIDE)
        here = pl.ds(pl.multiple_of(place[0] * QUARTER + (i // 4) * ROWS, ROWS), ROWS)
        gs = [x.astype(F32) for x in (g0[here, lanes], *(m[2, rows, lanes] for m in (m1, m2, m3)))]
        xs = [x[rows, lanes].astype(F32) for x in (x0, x1, x2, x3)]
        dattn = pair_sums(gs, xs, ones_ref[...])
        qs = [x.astype(F32) for x in (q0[here, lanes], *(m[0, rows, lanes] for m in (m1, m2, m3)))]
        ks = [x.astype(F32) for x in (k0[here, lanes], *(m[1, rows, lanes] for m in (m1, m2, m3)))]
        key_sums = [None] * 4
        for t in range(4):
            a = [attn[4 * t + u, rows, lanes].astype(F32) for u in range(4)]
            mean = sum(x * y for x, y in zip(a[1:], dattn[t][1:], strict=True)) + a[0] * dattn[t][0]
            query_sum = None
            for u in range(4):
                grad = a[u] * (dattn[t][u] - mean)
                query_sum = grad * ks[u] if query_sum is None else query_sum + grad * ks[u]
                term = grad * qs[t]
                key_sums[u] = term if key_sums[u] is None else key_sums[u] + term
            outs[t][0, rows, lanes] = (query_sum * SCALE).astype(BF16)
        for u in range(4):
            outs[u][1, rows, lanes] = (key_sums[u] * SCALE).astype(BF16)

    pl.loop(0, 16, unroll=4)(tile)


def time_second(place, q, k, g, m1, m2, m3, attn, x0, x1, x2, x3):
    piece = jax.ShapeDtypeStruct((2, QUARTER, D), BF16)
    return pl.pallas_call(
        time_second_kernel,
        in_specs=[SMEM_SPEC] + [VMEM_SPEC] * 11,
        out_specs=[VMEM_SPEC] * 4,
        out_shape=[piece] * 4,
        scratch_shapes=[pltpu.VMEM((2 * WIDE, WIDE), BF16)],
        compiler_params=kernel_params(24),
        cost_estimate=cost(1_000_000_000, 8 << 20),
        name="time_second",
    )(place, q, k, g, m1, m2, m3, attn, x0, x1, x2, x3)


def grad_rows(sg, place, pieces):
    for d, piece in enumerate(pieces):
        start = pl.multiple_of(lax.rem(place[0] + d, 4) * QUARTER, QUARTER)
        sg[pl.ds(start, QUARTER), :] = piece[...]


def deltas(sg_t, st_t):
    product = sg_t.astype(F32) * st_t.astype(F32)
    first = jnp.sum(product[:HD], axis=0, keepdims=True)
    second = jnp.sum(product[HD:], axis=0, keepdims=True)
    return jnp.concatenate(
        [first[:, :BLOCK], second[:, :BLOCK], first[:, BLOCK:], second[:, BLOCK:]], axis=1
    )


def back_sides_kernel(
    place, lists, q, from_low, from_high, probs, states_t, g0, g1, g2, g3, after,
    to_low, to_high, slopes, sg,
):
    low_ids, high_ids = listed(place, lists, 0), listed(place, lists, 1)
    grad_rows(sg, place, (g0, g1, g2, g3))

    def pair(p):
        lanes = pl.ds(pl.multiple_of(p * 128, 128), 128)
        rows = pl.ds(pl.multiple_of(p * 128, 128), 128)
        sg_p = sg[:, lanes]
        sg_t = transposed(sg_p)
        sg_cols = grouped_lanes(sg_t)
        q_cols = grouped_lanes((q[:, lanes].astype(F32) * SCALE).T.astype(BF16))
        delta = deltas(sg_t, states_t[rows, :])
        key_parts, value_parts = [], []
        for b in range(2):
            cols = slice(256 * b, 256 * b + 256)
            v_n = neighbour_rows(from_low.at[1], from_high.at[1], low_ids, high_ids, b, lanes)
            dp = dot(v_n, sg_cols[:, cols])
            pr = probs[p, :, cols]
            ds = (pr.astype(F32) * (dp - delta[:, cols])).astype(BF16)
            slopes[p, :, cols] = ds
            key_parts.append(dot_t(q_cols[:, cols], ds).T)
            value_parts.append(dot_t(sg_cols[:, cols], pr).T)
        for n, parts in enumerate((key_parts, value_parts)):
            for ids, out, side in ((low_ids, to_low, 0), (high_ids, to_high, 1)):
                for j in range(2):
                    total = sum(
                        jnp.where(ids[b] == j, parts[b][side * 128 : side * 128 + 128], 0.0)
                        for b in range(2)
                    )
                    out[n, j * 128 : j * 128 + 128, lanes] = total.astype(BF16)

    pl.loop(0, PAIRS, unroll=8)(pair)


def back_sides(place, lists, q, low, high, probs, states_t, pieces, after):
    message = jax.ShapeDtypeStruct((2, TOK, D), BF16)
    return pl.pallas_call(
        back_sides_kernel,
        in_specs=[SMEM_SPEC] * 2 + [VMEM_SPEC] * 9 + [ANY_SPEC],
        out_specs=[VMEM_SPEC] * 3,
        out_shape=[message, message, jax.ShapeDtypeStruct((PAIRS, TOK, 512), BF16)],
        scratch_shapes=[pltpu.VMEM((TOK, D), BF16)],
        compiler_params=kernel_params(32),
        cost_estimate=cost(6_000_000_000, 16 << 20),
        name="back_sides",
    )(place, lists, q, low, high, probs, states_t, *pieces, after)


def back_own_kernel(
    place, lists, q, k, v, from_high, from_low, weights, factors, states_t, slopes, g0, g1, g2, g3,
    query_grad, totals, sg,
):
    low_ids, high_ids = listed(place, lists, 0), listed(place, lists, 1)
    grad_rows(sg, place, (g0, g1, g2, g3))

    def pair(p):
        lanes = pl.ds(pl.multiple_of(p * 128, 128), 128)
        rows = pl.ds(pl.multiple_of(p * 128, 128), 128)
        sg_p = sg[:, lanes]
        sg_t = transposed(sg_p)
        q_rows = grouped_rows(q[:, lanes])
        factor = factors[p, 0:1, :]
        delta = deltas(sg_t, states_t[rows, :]) * factor
        scaled = grouped_lanes(sg_t).astype(F32) * factor
        sg_cols, sg_rows = scaled.astype(BF16), scaled.T.astype(BF16)
        k_t = transposed(k[:, lanes])
        dp = dot(v[:, lanes], sg_cols)
        pr = weights[p]
        ds = (pr.astype(F32) * (dp - delta)).astype(BF16)
        blocks = []
        for b in range(2):
            k_n_t = transposed(
                neighbour_rows(from_low.at[0], from_high.at[0], low_ids, high_ids, b, lanes)
            )
            for h in range(2):
                half, cols = slice(h * HD, h * HD + HD), slice(256 * b + 128 * h, 256 * b + 128 * h + 128)
                blocks.append(dot(k_t[half], ds[:, cols]) + dot(k_n_t[half], slopes[p, :, cols]))
        query_t = jnp.concatenate(
            [jnp.concatenate(blocks[:2], axis=0), jnp.concatenate(blocks[2:], axis=0)], axis=1
        )
        query_grad[:, lanes] = (query_t * SCALE).T.astype(BF16)
        totals[0, :, lanes] = dot(ds, q_rows) * SCALE
        totals[1, :, lanes] = dot(pr, sg_rows)

    pl.loop(0, PAIRS, unroll=8)(pair)


def back_own(place, lists, q, k, v, low, high, weights, factors, states_t, slopes, pieces):
    return pl.pallas_call(
        back_own_kernel,
        in_specs=[SMEM_SPEC] * 2 + [VMEM_SPEC] * 13,
        out_specs=[VMEM_SPEC] * 2,
        out_shape=[
            jax.ShapeDtypeStruct((TOK, D), BF16),
            jax.ShapeDtypeStruct((2, TOK, D), F32),
        ],
        scratch_shapes=[pltpu.VMEM((TOK, D), BF16)],
        compiler_params=kernel_params(32),
        cost_estimate=cost(6_000_000_000, 16 << 20),
        name="back_own",
    )(place, lists, q, k, v, high, low, weights, factors, states_t, slopes, *pieces)


def finish_time_kernel(place, t0, t1, t2, t3, query_t, key_t):
    for d, piece in enumerate((t0, t1, t2, t3)):
        start = pl.multiple_of(lax.rem(place[0] + d, 4) * QUARTER, QUARTER)
        query_t[pl.ds(start, QUARTER), :] = piece[0]
        key_t[pl.ds(start, QUARTER), :] = piece[1]


def finish_time(place, pieces):
    return pl.pallas_call(
        finish_time_kernel,
        in_specs=[SMEM_SPEC] + [VMEM_SPEC] * 4,
        out_specs=[VMEM_SPEC] * 2,
        out_shape=[jax.ShapeDtypeStruct((TOK, D), BF16)] * 2,
        compiler_params=kernel_params(24),
        cost_estimate=cost(0, 2 << 20),
        name="finish_time",
    )(place, *pieces)


def finish_kernel(totals, low, high, key_grad, value_grad):
    for n, out in ((0, key_grad), (1, value_grad)):
        out[...] = (totals[n] + low[n].astype(F32) + high[n].astype(F32)).astype(BF16)


def finish(totals, low, high):
    return pl.pallas_call(
        finish_kernel,
        in_specs=[VMEM_SPEC] * 3,
        out_specs=[VMEM_SPEC] * 2,
        out_shape=[jax.ShapeDtypeStruct((TOK, D), BF16)] * 2,
        compiler_params=kernel_params(24),
        cost_estimate=cost(0, 5 << 20),
        name="finish",
    )(totals, low, high)


def body(
    queries, key_vectors, value_vectors, query_time, key_time, out_grad, fluid_mask, occupancy, key_lists
):
    q, k, v = queries[0], key_vectors[0], value_vectors[0]
    qt, kt, og = query_time[0], key_time[0], out_grad[0]
    me, dom = lax.axis_index("tm"), lax.axis_index("space")
    place = jnp.stack([me, dom]).astype(jnp.int32)
    lists = lax.dynamic_index_in_dim(key_lists, dom, 0, keepdims=False)[:, :, 1].reshape(-1)
    occ = occupancy.reshape(-1, BLOCK)

    domains, steps = lax.axis_size("space"), lax.axis_size("tm")
    up = [(i, (i + 1) % domains) for i in range(domains)]
    down = [(i, (i - 1) % domains) for i in range(domains)]

    def shift(x, d):
        return lax.ppermute(x, "tm", [(i, (i + d) % steps) for i in range(steps)])

    m1, m2, m3, kv = stage(place, qt, kt, og, k, v)
    sent = (None, m1, m2, m3)
    arrived = {(4 - d) % 4: shift(sent[d], d) for d in (1, 3, 2)}
    ms = (arrived[1], arrived[2], arrived[3])
    low, high = lax.ppermute(kv, "space", up), lax.ppermute(kv, "space", down)

    weights, stats, partial = forward_own(place, fluid_mask, occ, q, k, v)
    *pieces, probs, states_t, factors = forward_sides(
        place, lists, fluid_mask, occ, q, low, high, stats, partial
    )
    *grads, attn = time_first(place, qt, kt, og, *ms, pieces[0])
    home = {(4 - d) % 4: shift(grads[d], d) for d in (1, 3, 2)}
    grad_pieces = (grads[0], home[1], home[2], home[3])

    there = {(4 - d) % 4: shift(pieces[d], d) for d in (1, 3, 2)}
    back = time_second(place, qt, kt, og, *ms, attn, pieces[0], there[1], there[2], there[3])

    to_low, to_high, slopes = back_sides(
        place, lists, q, low, high, probs, states_t, grad_pieces, back[0]
    )
    from_high = lax.ppermute(to_low, "space", down)
    from_low = lax.ppermute(to_high, "space", up)
    returned = {(4 - d) % 4: shift(back[d], d) for d in (1, 3, 2)}
    query_grad, totals = back_own(
        place, lists, q, k, v, low, high, weights, factors, states_t, slopes, grad_pieces
    )
    query_time_grad, key_time_grad = finish_time(
        place, (back[0], returned[1], returned[2], returned[3])
    )
    key_grad, value_grad = finish(totals, from_low, from_high)
    return tuple(
        x[None] for x in (query_grad, key_grad, value_grad, query_time_grad, key_time_grad)
    )


def solution(mesh):
    split = P("tm", "space", None)
    return jax.shard_map(
        body,
        mesh=mesh,
        in_specs=(split,) * 6 + (P(),) * 3,
        out_specs=(split,) * 5,
        check_vma=False,
    )
```

```python
import functools

import jax
import jax.numpy as jnp
from jax import lax
from jax.experimental import pallas as pl
from jax.experimental.pallas import tpu as pltpu
from jax.sharding import PartitionSpec as P

BLOCK = 128
H = 16
HD = 64
D = 1024
TOK = 256
QUARTER = 64
PAIRS = 8
SCALE = HD**-0.5
NEG = -1e30
F32 = jnp.float32
BF16 = jnp.bfloat16

VMEM_SPEC = pl.BlockSpec(memory_space=pltpu.VMEM)
ANY_SPEC = pl.BlockSpec(memory_space=pl.ANY)
HBM_SPEC = pl.BlockSpec(memory_space=pltpu.MemorySpace.HBM)
SMEM_SPEC = pl.BlockSpec(memory_space=pltpu.SMEM)


def dot(a, b):
    return jnp.dot(a, b, preferred_element_type=F32)


def dot_t(a, b):
    return lax.dot_general(a, b, (((1,), (1,)), ((), ())), preferred_element_type=F32)


def kernel_params(mib):
    return pltpu.CompilerParams(vmem_limit_bytes=mib * 1024 * 1024)


def cost(flops, nbytes):
    return pl.CostEstimate(flops=flops, bytes_accessed=nbytes, transcendentals=0)


def transposed(block):
    return block.astype(F32).T.astype(BF16)


def head_rows(block):
    row = lax.broadcasted_iota(jnp.int32, block.shape, 0)
    zero = jnp.zeros_like(block)
    return jnp.where(row < HD, block, zero), jnp.where(row < HD, zero, block)


def head_lanes(block):
    lane = lax.broadcasted_iota(jnp.int32, block.shape, 1)
    zero = jnp.zeros_like(block)
    return jnp.where(lane < HD, block, zero), jnp.where(lane < HD, zero, block)


def grouped_lanes(block_t):
    first, second = head_rows(block_t)
    return jnp.concatenate(
        [first[:, :BLOCK], second[:, :BLOCK], first[:, BLOCK:], second[:, BLOCK:]], axis=1
    )


def grouped_rows(block):
    first, second = head_lanes(block)
    return jnp.concatenate([first[:BLOCK], second[:BLOCK], first[BLOCK:], second[BLOCK:]], axis=0)


def stage_kernel(place, qt, kt, og, k, v, m1, m2, m3, kv, small, large, sems_in, sems_out):
    copies = []
    for d, out in ((1, m1), (3, m3), (2, m2)):
        start = pl.multiple_of(lax.rem(place[0] + d, 4) * QUARTER, QUARTER)
        for a, array in enumerate((qt, kt, og)):
            copies.append((array.at[pl.ds(start, QUARTER), :], small.at[3 * d - 3 + a], out.at[a]))
    copies += [(k, large.at[0], kv.at[0]), (v, large.at[1], kv.at[1])]
    ins = [pltpu.make_async_copy(a, b, sems_in.at[i]) for i, (a, b, c) in enumerate(copies)]
    outs = [pltpu.make_async_copy(b, c, sems_out.at[i]) for i, (a, b, c) in enumerate(copies)]
    for copy in ins:
        copy.start()
    for copy, after in zip(ins, outs, strict=True):
        copy.wait()
        after.start()
    for copy in outs:
        copy.wait()


def stage(place, *arrays):
    piece = jax.ShapeDtypeStruct((3, QUARTER, D), BF16)
    return pl.pallas_call(
        stage_kernel,
        in_specs=[SMEM_SPEC] + [HBM_SPEC] * 5,
        out_specs=[HBM_SPEC] * 4,
        out_shape=[piece] * 3 + [jax.ShapeDtypeStruct((2, TOK, D), BF16)],
        scratch_shapes=[
            pltpu.VMEM((9, QUARTER, D), BF16),
            pltpu.VMEM((2, TOK, D), BF16),
            pltpu.SemaphoreType.DMA((11,)),
            pltpu.SemaphoreType.DMA((11,)),
        ],
        compiler_params=kernel_params(60),
        cost_estimate=cost(0, 4 << 20),
        name="stage",
    )(place, *arrays)


def listed(place, lists, side):
    return [lists[b * 4 + 2 + side] for b in range(2)]


def neighbour_rows(low_ref, high_ref, low_ids, high_ids, b, lanes):
    low = low_ref[pl.ds(pl.multiple_of(low_ids[b] * BLOCK, BLOCK), BLOCK), lanes]
    high = high_ref[pl.ds(pl.multiple_of(high_ids[b] * BLOCK, BLOCK), BLOCK), lanes]
    return jnp.concatenate([low, high], axis=0)


def dead_column(occ, row_id, keep):
    dead = occ[pl.ds(row_id, 1), :].astype(F32)
    row = jnp.where((dead > 0.5) | jnp.logical_not(keep), NEG, 0.0)
    return jnp.broadcast_to(row, (BLOCK, BLOCK)).T


def pair_slice(p):
    return pl.ds(pl.multiple_of(p * 128, 128), 128)


def forward_own_kernel(place, fluid, occ, q, k, v, weights, stats, partial, bias):
    dom = place[1]
    for b in range(2):
        keep = fluid[dom * 2 + b] > 0
        for n in range(2):
            bias[b, n * 128 : n * 128 + 128] = dead_column(occ, dom * 2 + n, keep)

    def pair(p):
        lanes = pair_slice(p)
        q_cols = grouped_lanes((q[:, lanes].astype(F32) * SCALE).T.astype(BF16))
        v_t = transposed(v[:, lanes])
        scores = dot(k[:, lanes], q_cols)
        outs = []
        for g in range(4):
            cols = slice(g * 128, g * 128 + 128)
            s = scores[:, cols] + bias[g // 2]
            m = jnp.maximum(jnp.max(s, axis=0, keepdims=True), 0.0)
            e = jnp.exp(s - m)
            stats[p, 0:1, cols] = m
            stats[p, 1:2, cols] = jnp.sum(e, axis=0, keepdims=True)
            e = e.astype(BF16)
            weights[p, :, cols] = e
            outs.append(dot(v_t[(g % 2) * HD : (g % 2) * HD + HD], e))
        partial[pair_slice(p), :] = jnp.concatenate(
            [jnp.concatenate(outs[:2], axis=0), jnp.concatenate(outs[2:], axis=0)], axis=1
        )

    pl.loop(0, PAIRS, unroll=8)(pair)


def forward_own(place, fluid, occ, q, k, v):
    return pl.pallas_call(
        forward_own_kernel,
        in_specs=[SMEM_SPEC] * 2 + [VMEM_SPEC] * 4,
        out_specs=[VMEM_SPEC] * 3,
        out_shape=[
            jax.ShapeDtypeStruct((PAIRS, TOK, 512), BF16),
            jax.ShapeDtypeStruct((PAIRS, 8, 512), F32),
            jax.ShapeDtypeStruct((D, TOK), F32),
        ],
        scratch_shapes=[pltpu.VMEM((2, TOK, BLOCK), F32)],
        compiler_params=kernel_params(24),
        cost_estimate=cost(2_000_000_000, 8 << 20),
        name="forward_own",
    )(place, fluid, occ, q, k, v)


def forward_sides_kernel(
    place, lists, fluid, occ, q, low, high, stats, partial,
    states, p1, p2, p3, probs, states_t, factors, bias, scratch,
):
    me, dom = place[0], place[1]
    low_dom, high_dom = lax.rem(dom + 63, 64), lax.rem(dom + 1, 64)
    low_ids, high_ids = listed(place, lists, 0), listed(place, lists, 1)
    for b in range(2):
        keep = fluid[dom * 2 + b] > 0
        for h in (slice(0, 128), slice(128, 256)):
            bias[b, 0:128, h] = dead_column(occ, low_dom * 2 + low_ids[b], keep)
            bias[b, 128:256, h] = dead_column(occ, high_dom * 2 + high_ids[b], keep)

    def pair(p):
        lanes = pair_slice(p)
        q_cols = grouped_lanes((q[:, lanes].astype(F32) * SCALE).T.astype(BF16))
        outs = []
        for b in range(2):
            k_n = neighbour_rows(low.at[0], high.at[0], low_ids, high_ids, b, lanes)
            v_t = transposed(neighbour_rows(low.at[1], high.at[1], low_ids, high_ids, b, lanes))
            scores = dot(k_n, q_cols[:, 256 * b : 256 * b + 256])
            cols = slice(256 * b, 256 * b + 256)
            s = scores + bias[b]
            m_own, l_own = stats[p, 0:1, cols], stats[p, 1:2, cols]
            m = jnp.maximum(jnp.max(s, axis=0, keepdims=True), m_own)
            e = jnp.exp(s - m)
            scale_own = jnp.exp(m_own - m)
            total = jnp.exp(-m) + scale_own * l_own + jnp.sum(e, axis=0, keepdims=True)
            inv = 1.0 / total
            own = scale_own * inv
            factors[p, 0:1, cols] = own
            pr = (e * inv).astype(BF16)
            probs[p, :, cols] = pr
            halves = []
            for h in range(2):
                rows = pl.ds(pl.multiple_of(p * 128 + h * HD, HD), HD)
                half = slice(h * 128, h * 128 + 128)
                halves.append(
                    dot(v_t[h * HD : h * HD + HD], pr[:, half])
                    + partial[rows, b * 128 : b * 128 + 128] * own[:, half]
                )
            outs.append(jnp.concatenate(halves, axis=0))
        out_t = jnp.concatenate(outs, axis=1)
        states_t[pair_slice(p), :] = out_t.astype(BF16)
        scratch[:, lanes] = out_t.T.astype(BF16)

    pl.loop(0, PAIRS, unroll=8)(pair)
    for d, piece in ((0, states), (1, p1), (2, p2), (3, p3)):
        start = pl.multiple_of(lax.rem(me + d, 4) * QUARTER, QUARTER)
        piece[...] = scratch[pl.ds(start, QUARTER), :]


def forward_sides(place, lists, fluid, occ, q, low, high, stats, partial):
    piece = jax.ShapeDtypeStruct((QUARTER, D), BF16)
    return pl.pallas_call(
        forward_sides_kernel,
        in_specs=[SMEM_SPEC] * 3 + [VMEM_SPEC] * 6,
        out_specs=[VMEM_SPEC] * 7,
        out_shape=[piece] * 4
        + [
            jax.ShapeDtypeStruct((PAIRS, TOK, 512), BF16),
            jax.ShapeDtypeStruct((D, TOK), BF16),
            jax.ShapeDtypeStruct((PAIRS, 8, 512), F32),
        ],
        scratch_shapes=[pltpu.VMEM((2, TOK, TOK), F32), pltpu.VMEM((TOK, D), BF16)],
        compiler_params=kernel_params(24),
        cost_estimate=cost(2_000_000_000, 8 << 20),
        name="forward_sides",
    )(place, lists, fluid, occ, q, low, high, stats, partial)


ROWS = 16
WIDE = 256


def head_sums():
    row = lax.broadcasted_iota(jnp.int32, (2 * WIDE, WIDE), 0) % WIDE
    lane = lax.broadcasted_iota(jnp.int32, (2 * WIDE, WIDE), 1)
    return jnp.where(row // HD == lane // HD, 1.0, 0.0).astype(BF16)


def pair_sums(left, right, ones):
    products = jnp.concatenate([a * b for a in left for b in right], axis=0)
    high = products.astype(BF16)
    low = (products - high.astype(F32)).astype(BF16)
    sums = dot(jnp.concatenate([high, low], axis=1), ones)
    return [[sums[(4 * t + u) * ROWS : (4 * t + u + 1) * ROWS] for u in range(4)] for t in range(4)]


def time_first_kernel(place, q0, k0, g0, m1, m2, m3, after, s0, s1, s2, s3, attn, ones_ref):
    ones_ref[...] = head_sums()
    outs = (s0, s1, s2, s3)

    def tile(i):
        rows = pl.ds(pl.multiple_of((i // 4) * ROWS, ROWS), ROWS)
        lanes = pl.ds(pl.multiple_of((i % 4) * WIDE, WIDE), WIDE)
        here = pl.ds(pl.multiple_of(place[0] * QUARTER + (i // 4) * ROWS, ROWS), ROWS)
        qs = [x.astype(F32) for x in (q0[here, lanes], *(m[0, rows, lanes] for m in (m1, m2, m3)))]
        ks = [x.astype(F32) for x in (k0[here, lanes], *(m[1, rows, lanes] for m in (m1, m2, m3)))]
        gs = [x.astype(F32) for x in (g0[here, lanes], *(m[2, rows, lanes] for m in (m1, m2, m3)))]
        scores = pair_sums([x * SCALE for x in qs], ks, ones_ref[...])
        sums = list(gs)
        for t in range(4):
            row = scores[t]
            top = jnp.maximum(jnp.maximum(row[0], row[1]), jnp.maximum(row[2], row[3]))
            exps = [jnp.exp(x - top) for x in row]
            inv = 1.0 / ((exps[0] + exps[1]) + (exps[2] + exps[3]))
            for u in range(4):
                a = exps[u] * inv
                attn[4 * t + u, rows, lanes] = a.astype(BF16)
                sums[u] = sums[u] + a * gs[t]
        for u in range(4):
            outs[u][rows, lanes] = sums[u].astype(BF16)

    pl.loop(0, 16, unroll=8)(tile)


def time_first(place, q, k, g, m1, m2, m3, after):
    piece = jax.ShapeDtypeStruct((QUARTER, D), BF16)
    return pl.pallas_call(
        time_first_kernel,
        in_specs=[SMEM_SPEC] + [VMEM_SPEC] * 6 + [ANY_SPEC],
        out_specs=[VMEM_SPEC] * 5,
        out_shape=[piece] * 4 + [jax.ShapeDtypeStruct((16, QUARTER, D), BF16)],
        scratch_shapes=[pltpu.VMEM((2 * WIDE, WIDE), BF16)],
        compiler_params=kernel_params(24),
        cost_estimate=cost(1_000_000_000, 8 << 20),
        name="time_first",
    )(place, q, k, g, m1, m2, m3, after)


def time_second_kernel(
    place, q0, k0, g0, m1, m2, m3, attn, x0, x1, x2, x3, o0, o1, o2, o3, ones_ref
):
    ones_ref[...] = head_sums()
    outs = (o0, o1, o2, o3)

    def tile(i):
        rows = pl.ds(pl.multiple_of((i // 4) * ROWS, ROWS), ROWS)
        lanes = pl.ds(pl.multiple_of((i % 4) * WIDE, WIDE), WIDE)
        here = pl.ds(pl.multiple_of(place[0] * QUARTER + (i // 4) * ROWS, ROWS), ROWS)
        gs = [x.astype(F32) for x in (g0[here, lanes], *(m[2, rows, lanes] for m in (m1, m2, m3)))]
        xs = [x[rows, lanes].astype(F32) for x in (x0, x1, x2, x3)]
        dattn = pair_sums(gs, xs, ones_ref[...])
        qs = [x.astype(F32) for x in (q0[here, lanes], *(m[0, rows, lanes] for m in (m1, m2, m3)))]
        ks = [x.astype(F32) for x in (k0[here, lanes], *(m[1, rows, lanes] for m in (m1, m2, m3)))]
        key_sums = [None] * 4
        for t in range(4):
            a = [attn[4 * t + u, rows, lanes].astype(F32) for u in range(4)]
            mean = sum(x * y for x, y in zip(a[1:], dattn[t][1:], strict=True)) + a[0] * dattn[t][0]
            query_sum = None
            for u in range(4):
                grad = a[u] * (dattn[t][u] - mean)
                query_sum = grad * ks[u] if query_sum is None else query_sum + grad * ks[u]
                term = grad * qs[t]
                key_sums[u] = term if key_sums[u] is None else key_sums[u] + term
            outs[t][0, rows, lanes] = (query_sum * SCALE).astype(BF16)
        for u in range(4):
            outs[u][1, rows, lanes] = (key_sums[u] * SCALE).astype(BF16)

    pl.loop(0, 16, unroll=8)(tile)


def time_second(place, q, k, g, m1, m2, m3, attn, x0, x1, x2, x3):
    piece = jax.ShapeDtypeStruct((2, QUARTER, D), BF16)
    return pl.pallas_call(
        time_second_kernel,
        in_specs=[SMEM_SPEC] + [VMEM_SPEC] * 11,
        out_specs=[VMEM_SPEC] * 4,
        out_shape=[piece] * 4,
        scratch_shapes=[pltpu.VMEM((2 * WIDE, WIDE), BF16)],
        compiler_params=kernel_params(24),
        cost_estimate=cost(1_000_000_000, 8 << 20),
        name="time_second",
    )(place, q, k, g, m1, m2, m3, attn, x0, x1, x2, x3)


def grad_rows(sg, place, pieces):
    for d, piece in enumerate(pieces):
        start = pl.multiple_of(lax.rem(place[0] + d, 4) * QUARTER, QUARTER)
        sg[pl.ds(start, QUARTER), :] = piece[...]


def deltas(sg_t, st_t):
    product = sg_t.astype(F32) * st_t.astype(F32)
    first = jnp.sum(product[:HD], axis=0, keepdims=True)
    second = jnp.sum(product[HD:], axis=0, keepdims=True)
    return jnp.concatenate(
        [first[:, :BLOCK], second[:, :BLOCK], first[:, BLOCK:], second[:, BLOCK:]], axis=1
    )


def back_sides_kernel(
    place, lists, q, from_low, from_high, probs, states_t, g0, g1, g2, g3, after,
    to_low, to_high, slopes, sg,
):
    low_ids, high_ids = listed(place, lists, 0), listed(place, lists, 1)
    grad_rows(sg, place, (g0, g1, g2, g3))

    def pair(p):
        lanes = pl.ds(pl.multiple_of(p * 128, 128), 128)
        rows = pl.ds(pl.multiple_of(p * 128, 128), 128)
        sg_p = sg[:, lanes]
        sg_t = transposed(sg_p)
        sg_cols = grouped_lanes(sg_t)
        q_cols = grouped_lanes((q[:, lanes].astype(F32) * SCALE).T.astype(BF16))
        delta = deltas(sg_t, states_t[rows, :])
        key_parts, value_parts = [], []
        for b in range(2):
            cols = slice(256 * b, 256 * b + 256)
            v_n = neighbour_rows(from_low.at[1], from_high.at[1], low_ids, high_ids, b, lanes)
            dp = dot(v_n, sg_cols[:, cols])
            pr = probs[p, :, cols]
            ds = (pr.astype(F32) * (dp - delta[:, cols])).astype(BF16)
            slopes[p, :, cols] = ds
            key_parts.append(dot_t(q_cols[:, cols], ds).T)
            value_parts.append(dot_t(sg_cols[:, cols], pr).T)
        for n, parts in enumerate((key_parts, value_parts)):
            for ids, out, side in ((low_ids, to_low, 0), (high_ids, to_high, 1)):
                for j in range(2):
                    total = sum(
                        jnp.where(ids[b] == j, parts[b][side * 128 : side * 128 + 128], 0.0)
                        for b in range(2)
                    )
                    out[n, j * 128 : j * 128 + 128, lanes] = total.astype(BF16)

    pl.loop(0, PAIRS, unroll=8)(pair)


def back_sides(place, lists, q, low, high, probs, states_t, pieces, after):
    message = jax.ShapeDtypeStruct((2, TOK, D), BF16)
    return pl.pallas_call(
        back_sides_kernel,
        in_specs=[SMEM_SPEC] * 2 + [VMEM_SPEC] * 9 + [ANY_SPEC],
        out_specs=[VMEM_SPEC] * 3,
        out_shape=[message, message, jax.ShapeDtypeStruct((PAIRS, TOK, 512), BF16)],
        scratch_shapes=[pltpu.VMEM((TOK, D), BF16)],
        compiler_params=kernel_params(32),
        cost_estimate=cost(6_000_000_000, 16 << 20),
        name="back_sides",
    )(place, lists, q, low, high, probs, states_t, *pieces, after)


def back_own_kernel(
    place, lists, q, k, v, from_high, from_low, weights, factors, states_t, slopes, g0, g1, g2, g3,
    query_grad, totals, sg,
):
    low_ids, high_ids = listed(place, lists, 0), listed(place, lists, 1)
    grad_rows(sg, place, (g0, g1, g2, g3))

    def pair(p):
        lanes = pl.ds(pl.multiple_of(p * 128, 128), 128)
        rows = pl.ds(pl.multiple_of(p * 128, 128), 128)
        sg_p = sg[:, lanes]
        sg_t = transposed(sg_p)
        q_rows = grouped_rows(q[:, lanes])
        factor = factors[p, 0:1, :]
        delta = deltas(sg_t, states_t[rows, :]) * factor
        scaled = grouped_lanes(sg_t).astype(F32) * factor
        sg_cols, sg_rows = scaled.astype(BF16), scaled.T.astype(BF16)
        k_t = transposed(k[:, lanes])
        dp = dot(v[:, lanes], sg_cols)
        pr = weights[p]
        ds = (pr.astype(F32) * (dp - delta)).astype(BF16)
        blocks = []
        for b in range(2):
            k_n_t = transposed(
                neighbour_rows(from_low.at[0], from_high.at[0], low_ids, high_ids, b, lanes)
            )
            for h in range(2):
                half, cols = slice(h * HD, h * HD + HD), slice(256 * b + 128 * h, 256 * b + 128 * h + 128)
                blocks.append(dot(k_t[half], ds[:, cols]) + dot(k_n_t[half], slopes[p, :, cols]))
        query_t = jnp.concatenate(
            [jnp.concatenate(blocks[:2], axis=0), jnp.concatenate(blocks[2:], axis=0)], axis=1
        )
        query_grad[:, lanes] = (query_t * SCALE).T.astype(BF16)
        totals[0, :, lanes] = dot(ds, q_rows) * SCALE
        totals[1, :, lanes] = dot(pr, sg_rows)

    pl.loop(0, PAIRS, unroll=8)(pair)


def back_own(place, lists, q, k, v, low, high, weights, factors, states_t, slopes, pieces):
    return pl.pallas_call(
        back_own_kernel,
        in_specs=[SMEM_SPEC] * 2 + [VMEM_SPEC] * 13,
        out_specs=[VMEM_SPEC] * 2,
        out_shape=[
            jax.ShapeDtypeStruct((TOK, D), BF16),
            jax.ShapeDtypeStruct((2, TOK, D), F32),
        ],
        scratch_shapes=[pltpu.VMEM((TOK, D), BF16)],
        compiler_params=kernel_params(32),
        cost_estimate=cost(6_000_000_000, 16 << 20),
        name="back_own",
    )(place, lists, q, k, v, high, low, weights, factors, states_t, slopes, *pieces)


def finish_time_kernel(place, t0, t1, t2, t3, query_t, key_t, sems):
    copies = []
    for d, piece in enumerate((t0, t1, t2, t3)):
        rows = pl.ds(pl.multiple_of(lax.rem(place[0] + d, 4) * QUARTER, QUARTER), QUARTER)
        for n, out in enumerate((query_t, key_t)):
            copies.append(pltpu.make_async_copy(piece.at[n], out.at[rows, :], sems.at[2 * d + n]))
    for copy in copies:
        copy.start()
    for copy in copies:
        copy.wait()


def finish_time(place, pieces):
    return pl.pallas_call(
        finish_time_kernel,
        in_specs=[SMEM_SPEC] + [VMEM_SPEC] * 4,
        out_specs=[HBM_SPEC] * 2,
        out_shape=[jax.ShapeDtypeStruct((TOK, D), BF16)] * 2,
        scratch_shapes=[pltpu.SemaphoreType.DMA((8,))],
        compiler_params=kernel_params(24),
        cost_estimate=cost(0, 2 << 20),
        name="finish_time",
    )(place, *pieces)


def finish_kernel(totals, low, high, key_grad, value_grad):
    for n, out in ((0, key_grad), (1, value_grad)):
        out[...] = (totals[n] + low[n].astype(F32) + high[n].astype(F32)).astype(BF16)


def finish(totals, low, high):
    return pl.pallas_call(
        finish_kernel,
        in_specs=[VMEM_SPEC] * 3,
        out_specs=[VMEM_SPEC] * 2,
        out_shape=[jax.ShapeDtypeStruct((TOK, D), BF16)] * 2,
        compiler_params=kernel_params(24),
        cost_estimate=cost(0, 5 << 20),
        name="finish",
    )(totals, low, high)


def body(
    queries, key_vectors, value_vectors, query_time, key_time, out_grad, fluid_mask, occupancy, key_lists
):
    q, k, v = queries[0], key_vectors[0], value_vectors[0]
    qt, kt, og = query_time[0], key_time[0], out_grad[0]
    me, dom = lax.axis_index("tm"), lax.axis_index("space")
    place = jnp.stack([me, dom]).astype(jnp.int32)
    lists = lax.dynamic_index_in_dim(key_lists, dom, 0, keepdims=False)[:, :, 1].reshape(-1)
    occ = occupancy.reshape(-1, BLOCK)

    domains, steps = lax.axis_size("space"), lax.axis_size("tm")
    up = [(i, (i + 1) % domains) for i in range(domains)]
    down = [(i, (i - 1) % domains) for i in range(domains)]

    def shift(x, d):
        return lax.ppermute(x, "tm", [(i, (i + d) % steps) for i in range(steps)])

    m1, m2, m3, kv = stage(place, qt, kt, og, k, v)
    sent = (None, m1, m2, m3)
    arrived = {(4 - d) % 4: shift(sent[d], d) for d in (1, 3, 2)}
    ms = (arrived[1], arrived[2], arrived[3])
    low, high = lax.ppermute(kv, "space", up), lax.ppermute(kv, "space", down)

    weights, stats, partial = forward_own(place, fluid_mask, occ, q, k, v)
    *pieces, probs, states_t, factors = forward_sides(
        place, lists, fluid_mask, occ, q, low, high, stats, partial
    )
    *grads, attn = time_first(place, qt, kt, og, *ms, pieces[0])
    home = {(4 - d) % 4: shift(grads[d], d) for d in (1, 3, 2)}
    grad_pieces = (grads[0], home[1], home[2], home[3])

    there = {(4 - d) % 4: shift(pieces[d], d) for d in (1, 3, 2)}
    back = time_second(place, qt, kt, og, *ms, attn, pieces[0], there[1], there[2], there[3])

    to_low, to_high, slopes = back_sides(
        place, lists, q, low, high, probs, states_t, grad_pieces, back[0]
    )
    from_high = lax.ppermute(to_low, "space", down)
    from_low = lax.ppermute(to_high, "space", up)
    returned = {(4 - d) % 4: shift(back[d], d) for d in (1, 3, 2)}
    query_grad, totals = back_own(
        place, lists, q, k, v, low, high, weights, factors, states_t, slopes, grad_pieces
    )
    query_time_grad, key_time_grad = finish_time(
        place, (back[0], returned[1], returned[2], returned[3])
    )
    key_grad, value_grad = finish(totals, from_low, from_high)
    return tuple(
        x[None] for x in (query_grad, key_grad, value_grad, query_time_grad, key_time_grad)
    )


def solution(mesh):
    split = P("tm", "space", None)
    return jax.shard_map(
        body,
        mesh=mesh,
        in_specs=(split,) * 6 + (P(),) * 3,
        out_specs=(split,) * 5,
        check_vma=False,
    )
```
